256 devices in a mesh: ctx: 16 (over x, z_lo, core), ep: 16 (over z_hi, y).
Axes of the slice: x: 4, y: 4, z: 8 (z_hi: 4, z_lo: 2; z = z_hi * 2 + z_lo), core: 2. Of those that a mesh axis runs over, the one named last changes fastest.
Arguments:
- queries: bfloat16 [1024, 128, 576], P('ctx', 'ep'), may hold values from -24 to 24
- latents: bfloat16 [4096, 576], P('ctx'), may hold values from -6 to 6
- value_up: bfloat16 [128, 512, 128], P('ep'), may hold values from -0.25 to 0.25
- out_proj: bfloat16 [16384, 7168], P('ep', 'ctx'), may hold values from -0.375 to 0.375
- residual: bfloat16 [1024, 7168], P('ep', 'ctx'), may hold values from -6 to 6
- expert_gate: bfloat16 [16, 7168, 2048], P('ep', None, 'ctx'), may hold values from -0.0625 to 0.0625
- expert_up: bfloat16 [16, 7168, 2048], P('ep', None, 'ctx'), may hold values from -0.0625 to 0.0625
- expert_down: bfloat16 [16, 2048, 7168], P('ep', 'ctx'), may hold values from -0.125 to 0.125
- route_ids: int32 [1024, 8], P('ep'), may hold values from 0 to 15, all different within a row; in each aligned block of 64 rows (0 to 63, 64 to 127, ...) at most 36 rows name the same one
- route_gates: float32 [1024, 8], P('ep'), may hold values from 0.1 to 0.5
Outputs:
- layer_out: bfloat16 [1024, 7168], P('ep', 'ctx')
The draws below stay inside these ranges and needn't reach their ends.
Inputs may be any that keep to these rules, and one draw needn't show every extreme that they name: `route_ids`: in every aligned block of 64 rows (the rows of one index of ep) no expert is named more than 36 times, a bound that some block reaches.
All inputs are finite; a program needn't handle non-finite values.
Results may differ from the reference program's by a relative error of at most 0.03.
Values may be sent and summed in bfloat16 or wider, within the bound.
No kernel may reach another device: no remote copies, remote signals or barrier semaphores. Data moves between devices by JAX's collectives and lax.ppermute only.
A program may use at most 128 MiB of HBM per device.

```python
import math
import jax
import jax.numpy as jnp
import numpy as np
from jax import lax

D = 7168
FF = 2048
HEADS = 128
LATENT = 512
ROPE = 64
V_HEAD = 128
TOPK = 8
TOK_CTX = 64
LAT_DEV = 256
EXPERTS = 16
WIN = 1024
CTX = 4096
TOK_MOE = 64
CAP = 36
N_CTX = 16
N_EP = 16


def draw_queries(key, part):
    shape = (WIN, HEADS, LATENT + ROPE)
    key = jax.random.fold_in(key, 7)
    full = jnp.clip(jax.random.normal(key, shape, jnp.float32), -6.0, 6.0)
    return full.astype(jnp.bfloat16)


def draw_latents(key, part):
    shape = (CTX, LATENT + ROPE)
    key = jax.random.fold_in(key, 5)
    full = jnp.clip(jax.random.normal(key, shape, jnp.float32), -6.0, 6.0)
    return full.astype(jnp.bfloat16)


def level_of(rng, extent, pieces, least, top_value):
    def one(position, parts):
        draws = jax.random.uniform(jax.random.fold_in(jax.random.fold_in(rng, 6), position), (parts,), jnp.float32, least / len(pieces), top_value / len(pieces))
        return jnp.repeat(jnp.exp(draws), extent[position] // parts).reshape((-1,) + (1,) * (len(extent) - position - 1))

    factor_of = one(*pieces[0])
    for cut in pieces[1:]:
        factor_of = factor_of * one(*cut)
    return factor_of


def shared_out(key, own, number, rows, count, top, reach, lean):
    ranking = jax.random.permutation(key, count)
    crowded, common = load_shares(count, rows * top, reach, lean, True), load_shares(count, rows * top, reach, lean, False)
    places = jnp.arange(count)

    def named(lengths, offset_by):
        used = int((lengths > 0).sum())
        fixed = max(1, used // 4)
        moved = fixed + (places - fixed + offset_by * (used - fixed)) % max(1, count - fixed)
        return jnp.zeros((count,), jnp.int32).at[ranking[jnp.where(places < fixed, places, moved)]].set(jnp.asarray(lengths, jnp.int32))

    lengths = jnp.where(number % 4 == 0, named(crowded, number // 4), named(common, number - number // 4 - 1))
    mixed = jax.random.permutation(jax.random.fold_in(own, 3), count)
    source_of, taker = mixed[0:count // 2 * 2:2], mixed[1:count // 2 * 2:2]
    slack = jnp.minimum(lengths[source_of] - 1, reach - lengths[taker]) // 2
    slack = jnp.where((source_of == ranking[0]) | (taker == ranking[0]) | (lengths[taker] == 0), 0, jnp.maximum(slack, 0))
    moved = jax.random.randint(jax.random.fold_in(own, 4), (count // 2,), 0, 1 << 20) % (slack + 1)
    lengths = lengths.at[source_of].add(-moved).at[taker].add(moved)
    labels = jnp.searchsorted(jnp.cumsum(lengths), jnp.arange(rows * top), side="right").astype(jnp.int32)
    grid = labels.reshape(top, rows).T
    grid = grid[jax.random.permutation(jax.random.fold_in(own, 1), rows)]
    offset_by = jax.random.randint(jax.random.fold_in(own, 2), (rows, 1), 0, top)
    return jnp.take_along_axis(grid, (jnp.arange(top)[None, :] + offset_by) % top, axis=1)


def load_shares(number_of, total, bound, lean, full):
    loads = [(1 << 20) // math.isqrt(standing ** lean) + 1 for standing in range(1, number_of + 1)]
    largest = bound if full else min(bound, max(-(-total // number_of), total * loads[0] // sum(loads)))
    least = 1 if total - largest >= number_of - 1 else 0
    counts, rest = [largest] + [least] * (number_of - 1), total - largest - least * (number_of - 1)
    while rest > 0:
        movable = [i for i in range(1, number_of) if counts[i] < largest] or [i for i in range(1, number_of) if counts[i] < bound]
        mass, left = sum([loads[i] for i in movable]), rest
        for i in movable:
            extra = min(bound - counts[i], max(1, left * loads[i] // mass), rest)
            counts[i] = counts[i] + extra
            rest = rest - extra
    return np.array(counts)


def noise(own_key, extent, spread, bound, cuts=(), held_as=jnp.bfloat16):
    result = jax.random.normal(own_key, extent, jnp.float32) * spread
    if len(cuts) > 0:
        result = level_of(own_key, extent, cuts, -0.22, 0.18) * result
    return jnp.clip(result, min=-bound, max=bound).astype(held_as)


def setup_inputs(seed: int = 0) -> dict:
    keys = jax.random.split(jax.random.key(seed), 11)
    queries = draw_queries(jax.random.fold_in(keys[10], 71), 0)
    latents = draw_latents(jax.random.fold_in(keys[10], 71), 0)
    value_up = noise(keys[2], (HEADS, LATENT, V_HEAD), LATENT ** -0.5, 0.25, ((0, 16),))
    out_proj = noise(keys[3], (HEADS * V_HEAD, D), (8.0 / (HEADS * V_HEAD) ** 0.5), 0.375, ((0, 16), (1, 16)))
    residual = noise(keys[4], (WIN, D), 1.0, 6.0, ((0, 16), (1, 16)))
    expert_gate = noise(keys[5], (EXPERTS, D, FF), D ** -0.5, 0.0625, ((0, 16), (2, 16)))
    expert_up = noise(keys[6], (EXPERTS, D, FF), D ** -0.5, 0.0625, ((0, 16), (2, 16)))
    expert_down = noise(keys[7], (EXPERTS, FF, D), FF ** -0.5, 0.125, ((0, 16), (1, 16)))
    route_ids_keys = jax.random.split(jax.random.fold_in(keys[8], 1), WIN // TOK_MOE)
    route_ids_turns = jax.random.permutation(jax.random.fold_in(keys[8], 3), WIN // TOK_MOE)
    route_ids = jax.vmap(lambda own, number: shared_out(jax.random.fold_in(keys[8], 2), own, number, TOK_MOE, EXPERTS, TOPK, CAP, 2))(route_ids_keys, route_ids_turns).reshape((WIN, TOPK))
    route_gates = jnp.clip(0.1 + 0.4 * jax.random.uniform(keys[9], (WIN, TOPK), jnp.float32) ** level_of(keys[9], (WIN, TOPK), ((0, 16),), -0.2, 0.2), 0.1, 0.5)
    return dict(queries=queries, latents=latents, value_up=value_up, out_proj=out_proj, residual=residual, expert_gate=expert_gate, expert_up=expert_up, expert_down=expert_down, route_ids=route_ids, route_gates=route_gates)


NEG = -1.0e30


def reference(queries, latents, value_up, out_proj, residual, expert_gate, expert_up, expert_down, route_ids, route_gates):
    scale = (V_HEAD + ROPE) ** -0.5
    window = TOK_CTX * N_CTX
    context_len = LAT_DEV * N_CTX
    positions = context_len - window + jnp.arange(window, dtype=jnp.int32)
    key_pos = jnp.arange(context_len, dtype=jnp.int32)
    live = key_pos[None, :] <= positions[:, None]
    values = latents[:, :LATENT]

    def one_head(pair):
        head_queries, head_weight = pair
        scores = jnp.dot(head_queries, latents.T, preferred_element_type=jnp.float32) * scale
        scores = jnp.where(live, scores, NEG)
        running_max = jnp.max(scores, axis=1, keepdims=True)
        raised = jnp.exp(scores - running_max)
        total = jnp.sum(raised, axis=1, keepdims=True)
        numerator = jnp.dot(raised.astype(jnp.bfloat16), values, preferred_element_type=jnp.float32)
        context = (numerator / total).astype(jnp.bfloat16)
        return jnp.dot(context, head_weight, preferred_element_type=jnp.float32).astype(jnp.bfloat16)

    heads = lax.map(one_head, (jnp.transpose(queries, (1, 0, 2)), value_up))
    flat = jnp.transpose(heads, (1, 0, 2)).reshape(window, HEADS * V_HEAD)
    attended = jnp.dot(flat, out_proj, preferred_element_type=jnp.float32)
    moe_input = (residual.astype(jnp.float32) + attended).astype(jnp.bfloat16)

    tok_block = window // N_EP
    route_table = route_ids.reshape(N_EP, tok_block * TOPK)
    one_hot = (route_table[:, :, None] == jnp.arange(EXPERTS, dtype=jnp.int32)[None, None, :]).astype(jnp.int32)
    before = jnp.cumsum(one_hot, axis=1) - one_hot
    slots = jnp.sum(before * one_hot, axis=2).reshape(-1)
    sources = jnp.broadcast_to(jnp.arange(N_EP, dtype=jnp.int32)[:, None], route_table.shape).reshape(-1)
    chosen = route_table.reshape(-1)
    token_rows = jnp.repeat(moe_input, TOPK, axis=0)
    buffer = jnp.zeros((EXPERTS, N_EP, CAP, D), jnp.bfloat16).at[chosen, sources, slots].set(token_rows)
    slice_width = FF // N_CTX

    def one_expert(group):
        slot_rows, gate_weight, up_weight, down_weight = group
        slot_rows = slot_rows.reshape(N_EP * CAP, D)
        gated = jnp.dot(slot_rows, gate_weight, preferred_element_type=jnp.float32)
        upward = jnp.dot(slot_rows, up_weight, preferred_element_type=jnp.float32)
        hidden = (jax.nn.silu(gated) * upward).astype(jnp.bfloat16)
        hidden_slices = jnp.transpose(hidden.reshape(N_EP * CAP, N_CTX, slice_width), (1, 0, 2))
        down_slices = down_weight.reshape(N_CTX, slice_width, D)

        def add_slice(accum, pair):
            part = jnp.dot(pair[0], pair[1], preferred_element_type=jnp.float32).astype(jnp.bfloat16)
            part = lax.optimization_barrier(part)
            return accum + part.astype(jnp.float32), None

        summed, _ = lax.scan(add_slice, jnp.zeros((N_EP * CAP, D), jnp.float32), (hidden_slices, down_slices))
        return summed.reshape(N_EP, CAP, D)

    outputs = lax.map(one_expert, (buffer, expert_gate, expert_up, expert_down))
    picked = outputs[chosen, sources, slots].reshape(window, TOPK, D)
    routed = jnp.sum(picked * route_gates[:, :, None], axis=1)
    return (moe_input.astype(jnp.float32) + routed).astype(jnp.bfloat16)
```

```python
import jax
import jax.numpy as jnp
from jax import lax
from jax.sharding import PartitionSpec as P

NEG = -1e30


def local(
    queries,
    latents,
    value_up,
    out_proj,
    residual,
    expert_gate,
    expert_up,
    expert_down,
    route_ids,
    route_gates,
):
    query_count, head_count, feature_width = queries.shape
    latent_rows = latents.shape[0]
    latent_width = value_up.shape[1]
    value_width = value_up.shape[2]
    scale = (value_width + feature_width - latent_width) ** (-0.5)
    ctx_devices = lax.axis_size("ctx")
    ep_devices = lax.axis_size("ep")
    window = query_count * ctx_devices
    first_pos = latent_rows * ctx_devices - window + lax.axis_index("ctx") * query_count
    query_pos = first_pos + jnp.arange(query_count, dtype=jnp.int32)
    row_pos = jnp.repeat(query_pos, head_count)
    query_rows = queries.reshape(query_count * head_count, feature_width)
    row_count = query_count * head_count
    padding = -feature_width % 128
    query_rows = jnp.pad(query_rows, ((0, 0), (0, padding)))
    piece = lax.all_gather(jnp.pad(latents, ((0, 0), (0, padding))), "ctx", axis=0, tiled=True)
    running_max = jnp.full((row_count,), NEG, jnp.float32)
    scores = jnp.einsum("qc,kc->qk", query_rows, piece, preferred_element_type=jnp.float32) * scale
    key_pos = jnp.arange(piece.shape[0], dtype=jnp.int32)
    scores = jnp.where(key_pos[None, :] <= row_pos[:, None], scores, NEG)
    new_max = jnp.maximum(running_max, jnp.max(scores, axis=1))
    raised = jnp.exp(scores - new_max[:, None])
    soft = raised.astype(jnp.bfloat16)
    added = jnp.dot(soft, piece[:, :latent_width], preferred_element_type=jnp.float32)
    total = jnp.sum(raised, axis=1)
    context = (
        (added / total[:, None]).astype(jnp.bfloat16).reshape(query_count, head_count, latent_width)
    )
    head_out = jnp.einsum(
        "thc,hcv->thv", context, value_up, preferred_element_type=jnp.float32
    ).astype(jnp.bfloat16)
    head_out = head_out.reshape(query_count, head_count * value_width)
    spread = jnp.dot(
        lax.all_gather(head_out, "ctx", axis=0, tiled=True),
        out_proj,
        preferred_element_type=jnp.float32,
    )
    arrived = lax.all_to_all(
        spread.astype(jnp.bfloat16).reshape(ep_devices, -1, spread.shape[1]),
        "ep",
        split_axis=0,
        concat_axis=0,
        tiled=True,
    )
    attended = jnp.sum(arrived.astype(jnp.float32), axis=0)
    moe_input = (residual.astype(jnp.float32) + attended).astype(jnp.bfloat16)
    token_count, pick_count = route_ids.shape
    experts = ep_devices * expert_gate.shape[0]
    capacity = min(
        token_count, token_count * pick_count // experts + token_count * pick_count // (8 * experts)
    )
    flat_routes = route_ids.reshape(token_count * pick_count)
    one_hot = (flat_routes[:, None] == jnp.arange(experts, dtype=jnp.int32)[None, :]).astype(
        jnp.int32
    )
    before = jnp.cumsum(one_hot, axis=0) - one_hot
    slots = jnp.sum(before * one_hot, axis=1)
    target = (flat_routes * capacity + slots).reshape(token_count, pick_count)
    places = jnp.arange(experts * capacity, dtype=jnp.int32)
    matched = target[:, :, None] == places[None, None, :]
    placing = jnp.transpose(jnp.any(matched, axis=1).astype(jnp.bfloat16))
    gate_weight = expert_gate[0]
    up_weight = expert_up[0]
    down_weight = expert_down[0]
    local_width = moe_input.shape[1]
    outgoing = jnp.dot(placing, moe_input, preferred_element_type=jnp.float32).astype(jnp.bfloat16)
    outgoing = outgoing.reshape(experts, capacity, local_width)
    arrived = lax.all_to_all(outgoing, "ep", split_axis=0, concat_axis=0, tiled=True)
    slot_rows = lax.all_gather(arrived.reshape(-1, local_width), "ctx", axis=0)
    gate_weight = gate_weight.reshape(ctx_devices, local_width, -1)
    up_weight = up_weight.reshape(ctx_devices, local_width, -1)
    gate_add = jnp.einsum("csf,cfh->sh", slot_rows, gate_weight, preferred_element_type=jnp.float32)
    up_add = jnp.einsum("csf,cfh->sh", slot_rows, up_weight, preferred_element_type=jnp.float32)
    hidden = (jax.nn.silu(gate_add) * up_add).astype(jnp.bfloat16)
    hidden_width = hidden.shape[1]
    down_blocks = jnp.transpose(
        down_weight.reshape(hidden_width, ctx_devices, local_width), (1, 0, 2)
    )
    down_blocks = lax.all_to_all(down_blocks, "ctx", split_axis=0, concat_axis=0, tiled=True)
    hidden = lax.all_gather(hidden, "ctx", axis=0)
    summed = jnp.einsum("csh,chf->sf", hidden, down_blocks, preferred_element_type=jnp.float32)
    summed = summed.reshape(arrived.shape[0], capacity, local_width)
    returned = lax.all_to_all(
        summed.astype(jnp.bfloat16), "ep", split_axis=0, concat_axis=0, tiled=True
    ).astype(summed.dtype)
    flat_returned = returned.reshape(experts * capacity, returned.shape[2])
    picked_rows = flat_returned[target]
    routed = jnp.sum(picked_rows * route_gates[:, :, None], axis=1)
    return (moe_input.astype(jnp.float32) + routed).astype(jnp.bfloat16)


def solution(mesh):
    return jax.shard_map(
        local,
        mesh=mesh,
        in_specs=(
            P("ctx", "ep", None),
            P("ctx", None),
            P("ep", None, None),
            P("ep", "ctx"),
            P("ep", "ctx"),
            P("ep", None, "ctx"),
            P("ep", None, "ctx"),
            P("ep", "ctx", None),
            P("ep", None),
            P("ep", None),
        ),
        out_specs=P("ep", "ctx"),
        check_vma=False,
    )
```

```python
import functools

import jax
import jax.numpy as jnp
from jax import lax
from jax.experimental import pallas as pl
from jax.experimental.pallas import tpu as pltpu
from jax.sharding import Mesh
from jax.sharding import PartitionSpec as P

NEG = -1e30
CTX = ("x", "z_lo", "core")
EP = ("z_hi", "y")
SIZES = {"x": 4, "z_lo": 2, "core": 2, "z_hi": 4, "y": 4}
CAPACITY = 36
F32, BF16 = jnp.float32, jnp.bfloat16
VMEM = pl.BlockSpec(memory_space=pltpu.VMEM)
SMEM = pl.BlockSpec(memory_space=pltpu.SMEM)


def shift(value, axis, by):
    size = SIZES[axis]
    return lax.ppermute(value, axis, [(i, (i + by) % size) for i in range(size)])


def permute(value, axes, source):
    first, second = (SIZES[axis] for axis in axes)
    pairs = []
    for i in range(first):
        for j in range(second):
            p, q = source(i, j)
            pairs.append((p * second + q, i * second + j))
    return lax.ppermute(value, axes, pairs)


def gather_plane(own):
    other = shift(own, "z_lo", 1)
    blocks = {}
    for dz, block in ((0, own), (1, other)):
        blocks[0, dz] = block
        for d in (1, 2, 3):
            blocks[d, dz] = shift(block, "x", d)
    return [blocks[key] for key in PLANE]


def gather_wide(own, together=None):
    first = shift(own, "z_lo", 1), shift(own, "x", 1), shift(own, "x", -1)
    if together is not None:
        first, together[:] = lax.optimization_barrier((first, together))
    other, before, after = first
    blocks = {(0, 0): own, (0, 1): other, (1, 0): before, (3, 0): after}
    blocks[1, 1] = shift(other, "x", 1)
    blocks[3, 1] = shift(other, "x", -1)
    blocks[2, 0] = shift(before, "x", 1)
    blocks[2, 1] = shift(blocks[3, 1], "x", -1)
    return [blocks[key] for key in PLANE]


PLANE = [(dx, dz) for dx in range(4) for dz in range(2)]
STEPS = [(0, 0), (0, 1), (1, 0), (1, 1)]
def call(kernel, outs, scratch=(), vmem=8 << 20, flops=0, scalars=1, name=None):
    def run(*args):
        return pl.pallas_call(
            kernel,
            out_shape=outs,
            in_specs=[SMEM] * scalars + [VMEM] * (len(args) - scalars),
            out_specs=jax.tree.map(lambda _: VMEM, outs),
            scratch_shapes=list(scratch),
            compiler_params=pltpu.CompilerParams(vmem_limit_bytes=vmem),
            cost_estimate=pl.CostEstimate(flops=flops, bytes_accessed=1 << 20, transcendentals=0),
            name=name,
        )(*args)

    return run


def dot(a, b, dims=((1,), (0,))):
    return lax.dot_general(a, b, (dims, ((), ())), preferred_element_type=F32)


def attend(scale, tokens, table, queries, value_up, *refs):
    blocks, out, scores = refs[:16], refs[16], refs[17]
    rows, _ = queries.shape
    keys = blocks[0].shape[1]
    heads, width, value_width = value_up.shape
    row_pos = table[16] + (lax.broadcasted_iota(jnp.int32, (rows, 1), 0) & (tokens - 1))
    lane = lax.broadcasted_iota(jnp.int32, (1, keys), 1)
    query = queries[...]
    top = jnp.full((rows, 128), NEG, F32)
    for i, block in enumerate(blocks):
        score = dot(query, block[...])
        score = jnp.where(table[i] * keys + lane <= row_pos, score, NEG)
        scores[:, i * keys : (i + 1) * keys] = score
        for j in range(0, keys, 128):
            top = jnp.maximum(top, score[:, j : j + 128])
    top = jnp.max(top, axis=1, keepdims=True)
    total = jnp.zeros((rows, 128), F32)
    added = jnp.zeros((rows, width), F32)
    for i, block in enumerate(blocks):
        raised = jnp.exp((scores[:, i * keys : (i + 1) * keys] - top) * scale)
        for j in range(0, keys, 128):
            total = total + raised[:, j : j + 128]
        added = added + dot(raised.astype(BF16), block[:width, :], ((1,), (1,)))
    context = (added / jnp.sum(total, axis=1, keepdims=True)).astype(BF16)
    for h in range(heads):
        head = dot(context[h * tokens : (h + 1) * tokens], value_up[h])
        out[:, h * value_width : (h + 1) * value_width] = head.astype(BF16)


def project(table, weight, swapped, *refs):
    blocks, outs, rows, sums = refs[:8], refs[8:12], refs[12], refs[13]
    count = blocks[0].shape[0]
    for i, block in enumerate(blocks):
        rows[pl.ds(pl.multiple_of(table[i] * count, count), count), :] = block[...]
    total = rows.shape[0]
    for which, columns in enumerate((weight, swapped)):
        sums[which * total : (which + 1) * total, :] = dot(
            rows[...], columns[...], ((1,), (1,))
        ).astype(BF16)
    half = total // 2
    for k, out in enumerate(outs):
        out[...] = sums[pl.ds(pl.multiple_of(table[8 + k] * half, half), half), :]


def add_parts(table, *refs):
    parts, outs = refs[:4], refs[4:]
    count = outs[0].shape[0]
    for d, out in enumerate(outs):
        at = pl.ds(pl.multiple_of(((table[0] + d) & 3) * count, count), count)
        total = parts[0][at, :].astype(F32)
        for part in parts[1:]:
            total = total + part[at, :].astype(F32)
        out[...] = total.astype(out.dtype)


def place(table, *refs):
    blocks, outs, choices, rows, routes = refs[:4], refs[4:8], refs[8], refs[9], refs[10]
    count = blocks[0].shape[0]
    width = rows.shape[1] // 2
    picks = (blocks[0].shape[1] - width) // 4
    for k, block in enumerate(blocks):
        at = pl.ds(pl.multiple_of(table[k] * count, count), count)

        @pl.when(table[4 + k] == 0)
        def _(at=at, block=block):
            rows[at, :width] = block[:, :width]
            routes[at, :] = block[:, width:].astype(F32)

        @pl.when(table[4 + k] == 1)
        def _(at=at, block=block):
            rows[at, width:] = block[:, :width]

    total = rows.shape[0]
    index = lax.broadcasted_iota(jnp.int32, (total, total), 0)
    other = lax.broadcasted_iota(jnp.int32, (total, total), 1)
    earlier = (other < index) & (other // count == index // count)
    earlier = jnp.where(earlier, 1.0, 0.0).astype(BF16)
    ids = routes[:, :picks]
    gates = routes[:, picks : 2 * picks] + (
        routes[:, 2 * picks : 3 * picks] + routes[:, 3 * picks :]
    )
    half = lax.broadcasted_iota(jnp.int32, (total, 1), 0) // count
    places = lax.broadcasted_iota(jnp.int32, (total, 2 * CAPACITY), 1).astype(F32)
    for d, out in enumerate(outs):
        match = ids == table[8 + d].astype(F32)
        hit = jnp.max(jnp.where(match, 1.0, 0.0), axis=1, keepdims=True)
        weight = jnp.sum(jnp.where(match, gates, 0.0), axis=1, keepdims=True)
        before = dot(earlier, jnp.broadcast_to(hit, (total, 128)).astype(BF16))[:, :1]
        slot = jnp.where(hit > 0.0, before + (half * CAPACITY).astype(F32), -1.0)
        choices[:, d : d + 1] = slot
        choices[:, 4 + d : 5 + d] = weight
        placing = jnp.where(places == slot, 1.0, 0.0).astype(BF16)
        out[...] = dot(placing, rows[...], ((0,), (0,))).astype(BF16)


def expand(before, table, *refs):
    sums, refs = (refs[0], refs[1:]) if before else (None, refs)
    weights, blocks, out = refs[:4], refs[4:-1], refs[-1]
    hidden = weights[0].shape[2]
    total = sums[...] if before else None
    for i, block in enumerate(blocks):
        weight = jnp.concatenate([weight[table[i]] for weight in weights], axis=1)
        term = dot(block[...], weight)
        total = term if total is None else total + term
    if not before:
        out[...] = total
        return
    for j in range(2):
        gated = total[:, 2 * j * hidden : (2 * j + 1) * hidden]
        upward = total[:, (2 * j + 1) * hidden : (2 * j + 2) * hidden]
        value = gated / (1.0 + jnp.exp(-gated)) * upward
        out[:, j * hidden : (j + 1) * hidden] = value.astype(BF16)


def regroup(table, weight, *outs):
    width = outs[0].shape[2]
    for j in range(8):
        for d, out in enumerate(outs):

            @pl.when(table[j] >> 1 == d)
            def _(j=j, out=out):
                out[table[j] & 1] = weight[:, j * width : (j + 1) * width]


def contract(near, far, other_near, other_far, *refs):
    blocks, outs = refs[:8], refs[8:]
    total = None
    for i, block in enumerate(blocks):
        own, other = (far, other_far) if i & 1 else (near, other_near)
        term = dot(block[...], jnp.concatenate([own[i >> 1], other[i >> 1]], axis=0))
        total = term if total is None else total + term
    part = outs[0].shape[0]
    for d, out in enumerate(outs):
        out[...] = total[d * part : (d + 1) * part].astype(BF16)


def combine(table, choices, *refs):
    parts, outs, sums = refs[:4], refs[4:8], refs[8]
    total = None
    places = lax.broadcasted_iota(jnp.int32, (choices.shape[0], 2 * CAPACITY), 1).astype(F32)
    for d, block in enumerate(parts):
        weight = jnp.where(places == choices[:, d : d + 1], choices[:, 4 + d : 5 + d], 0.0)
        high = weight.astype(BF16)
        low = (weight - high.astype(F32)).astype(BF16)
        term = dot(high, block[...]) + dot(low, block[...])
        total = term if total is None else total + term
    sums[...] = total
    count, width = outs[0].shape
    for k, out in enumerate(outs):
        at = pl.ds(pl.multiple_of(table[k] * count, count), count)

        @pl.when(table[4 + k] == 0)
        def _(at=at, out=out):
            out[...] = sums[at, :width].astype(BF16)

        @pl.when(table[4 + k] == 1)
        def _(at=at, out=out):
            out[...] = sums[at, width:].astype(BF16)


def struct(*shape, dtype=BF16):
    return jax.ShapeDtypeStruct(shape, dtype)


def tie(value, *others):
    return lax.optimization_barrier((value, *others))[0]


def local(
    queries,
    latents,
    value_up,
    out_proj,
    residual,
    expert_gate,
    expert_up,
    expert_down,
    route_ids,
    route_gates,
):
    tokens, heads, feature_width = queries.shape
    keys = latents.shape[0]
    value_width = value_up.shape[2]
    scale = (value_width + feature_width - value_up.shape[1]) ** (-0.5)
    width = out_proj.shape[1]
    x, z, core = (lax.axis_index(axis) for axis in CTX)
    plane, row = (lax.axis_index(axis) for axis in EP)
    chips = [(((x - dx) & 3), (z ^ dz)) for dx, dz in PLANE]
    owners = [cx * 4 + cz * 2 + (core ^ dk) for dk in range(2) for cx, cz in chips]
    me = x * 4 + z * 2 + core

    first = keys * 16 - tokens * 16 + me * tokens
    rows = jnp.transpose(queries, (1, 0, 2)).reshape(heads * tokens, feature_width)
    gathered = gather_wide(jnp.transpose(latents), [])
    hidden_width = expert_gate.shape[2]
    table = jnp.stack([(((j >> 1) - x) & 3) * 2 + (z ^ (j & 1)) for j in range(8)])
    down = call(regroup, [struct(2, hidden_width, 2 * width)] * 4, name="regroup")(
        table.astype(jnp.int32), expert_down[0]
    )
    down = list(down)
    gathered[6], rows, down[0] = lax.optimization_barrier((gathered[6], rows, down[0]))
    swapped = [shift(block, "core", 1) for block in gathered]
    out_weight = jnp.transpose(out_proj)
    out_swapped = shift(tie(out_weight, *gathered), "core", 1)
    gates = []
    rest = route_gates
    for _ in range(3):
        gates.append(rest.astype(BF16))
        rest = rest - gates[-1].astype(F32)
    routes = jnp.concatenate([route_ids.astype(BF16), *gates], axis=1)

    down[1] = shift(tie(down[1], *gathered), "x", 1)
    down[3] = shift(tie(down[3], *gathered), "x", 3)
    head_out = call(
        functools.partial(attend, scale, tokens),
        struct(tokens, heads * value_width),
        [pltpu.VMEM((heads * tokens, 16 * keys), F32)],
        vmem=20 << 20,
        flops=10 << 30,
        name="attend",
    )(jnp.stack(owners + [first]).astype(jnp.int32), rows, value_up, *gathered, *swapped)

    head_out, out_swapped, down[1], down[3] = lax.optimization_barrier(
        (head_out, out_swapped, down[1], down[3])
    )

    count = route_ids.shape[0]

    gathered_heads = gather_plane(head_out)
    table = [cz * 4 + cx for cx, cz in chips]
    table += [((row & 1) ^ k0 ^ core) * 2 + ((row >> 1) ^ k1) for k1, k0 in STEPS]
    parts = call(
        project,
        [struct(4 * tokens, width)] * 4,
        [
            pltpu.VMEM((8 * tokens, heads * value_width), BF16),
            pltpu.VMEM((16 * tokens, width), BF16),
        ],
        vmem=16 << 20,
        flops=2 << 30,
        name="project",
    )(
        jnp.stack(table).astype(jnp.int32),
        out_weight,
        out_swapped,
        *gathered_heads,
    )
    down[2] = shift(tie(down[2], parts[0]), "x", 2)
    parts = [
        permute(part, ("core", "y"), lambda c, y: (y & 1, ((y >> 1) ^ k1) * 2 + (c ^ k0)))
        for part, (k1, k0) in zip(parts, STEPS)
    ]
    plane_table = plane.reshape(1).astype(jnp.int32)
    sums = call(
        add_parts, [struct(count, width, dtype=F32)] + [struct(count, width)] * 3, name="add_parts"
    )(plane_table, *parts)
    down[2], *sums = lax.optimization_barrier((down[2], *sums))
    near = jnp.stack([block[0] for block in down])
    far = jnp.stack([block[1] for block in down])
    attended = sums[0]
    for d in (1, 2, 3):
        attended = attended + shift(sums[d], "z_hi", d).astype(F32)
    moe_input = (residual.astype(F32) + attended).astype(BF16)

    moe_input, near, far = lax.optimization_barrier((moe_input, near, far))

    routed_input = jnp.concatenate([moe_input, routes], axis=1)
    planes = [
        permute(
            routed_input,
            ("core", "z_hi"),
            lambda c, p: ((p >> 1) ^ k1, 2 * c + ((p & 1) ^ k0)),
        )
        for k1, k0 in STEPS
    ]
    table = [(plane & 1) ^ k0 for _, k0 in STEPS] + [(plane >> 1) ^ k1 for k1, _ in STEPS]
    table += [plane * 4 + ((row + d) & 3) for d in range(4)]
    *outgoing, choices = call(
        place,
        [struct(2 * CAPACITY, 2 * width)] * 4 + [struct(2 * count, 8, dtype=F32)],
        [pltpu.VMEM((2 * count, 2 * width), BF16), pltpu.VMEM((2 * count, routes.shape[1]), F32)],
        name="place",
    )(jnp.stack(table).astype(jnp.int32), *planes)
    arrived = [outgoing[0]] + [shift(outgoing[d], "y", d) for d in (1, 2, 3)]
    arrived = jnp.concatenate(arrived, axis=0)
    gate, up, near = lax.optimization_barrier((expert_gate, expert_up, near, arrived))[:3]
    gate = gate.reshape(8, 2 * width, hidden_width)
    up = up.reshape(8, 2 * width, hidden_width)
    swapped = [shift(gate, "core", 1), shift(up, "core", 1)]
    slots = gather_wide(arrived, swapped)
    gate_swapped, up_swapped = swapped
    far = shift(tie(far, slots[1]), "z_lo", 1)
    near_swapped = shift(tie(near, slots[1]), "core", 1)

    early, late = [0, 1, 2, 6, 7], [3, 4, 5]
    weights = (gate, up, gate_swapped, up_swapped)
    part = struct(8 * CAPACITY, 4 * hidden_width, dtype=F32)
    hidden = ()
    for some, out in ((early, part), (late, struct(8 * CAPACITY, 2 * hidden_width))):
        picks = [chips[i][0] * 2 + chips[i][1] for i in some]
        hidden = call(
            functools.partial(expand, len(hidden)),
            out,
            vmem=16 << 20,
            flops=len(some) * (512 << 20),
            name="expand",
        )(jnp.stack(picks).astype(jnp.int32), *hidden, *weights, *[slots[i] for i in some])
        hidden = (hidden,)
    (hidden,) = hidden
    hidden, near_swapped, far = lax.optimization_barrier((hidden, near_swapped, far))
    far_swapped = shift(far, "core", 1)
    hidden = gather_plane(hidden)
    results = call(
        contract,
        [struct(2 * CAPACITY, 2 * width)] * 4,
        scalars=0,
        vmem=16 << 20,
        flops=2 << 30,
        name="contract",
    )(near, far, near_swapped, far_swapped, *hidden)

    returned = [results[0]] + [shift(results[d], "y", -d) for d in (1, 2, 3)]
    table = [(plane & 1) ^ k0 for _, k0 in STEPS] + [(plane >> 1) ^ k1 for k1, _ in STEPS]
    sums = call(
        combine,
        [struct(count, width)] * 4,
        [pltpu.VMEM((2 * count, 2 * width), F32)],
        name="combine",
    )(jnp.stack(table).astype(jnp.int32), choices, *returned)
    routed = None
    for part, (k1, k0) in zip(sums, STEPS):
        part = permute(
            part,
            ("core", "z_hi"),
            lambda c, p: (p >> 1, ((c ^ k1) << 1) | ((p & 1) ^ k0)),
        ).astype(F32)
        routed = part if routed is None else routed + part
    return (moe_input.astype(F32) + routed).astype(BF16)


def solution(mesh):
    split = Mesh(mesh.devices.reshape(tuple(SIZES.values())), tuple(SIZES))
    return jax.shard_map(
        local,
        mesh=split,
        in_specs=(
            P(CTX, EP, None),
            P(CTX, None),
            P(EP, None, None),
            P(EP, CTX),
            P(EP, CTX),
            P(EP, None, CTX),
            P(EP, None, CTX),
            P(EP, CTX, None),
            P(EP, None),
            P(EP, None),
        ),
        out_specs=P(EP, CTX),
        check_vma=False,
    )
```

```python
import functools

import jax
import jax.numpy as jnp
from jax import lax
from jax.experimental import pallas as pl
from jax.experimental.pallas import tpu as pltpu
from jax.sharding import Mesh
from jax.sharding import PartitionSpec as P

NEG = -1e30
CTX = ("x", "z_lo", "core")
EP = ("z_hi", "y")
SIZES = {"x": 4, "z_lo": 2, "core": 2, "z_hi": 4, "y": 4}
CAPACITY = 36
F32, BF16 = jnp.float32, jnp.bfloat16
VMEM = pl.BlockSpec(memory_space=pltpu.VMEM)
SMEM = pl.BlockSpec(memory_space=pltpu.SMEM)


def shift(value, axis, by):
    size = SIZES[axis]
    return lax.ppermute(value, axis, [(i, (i + by) % size) for i in range(size)])


def permute(value, axes, source):
    first, second = (SIZES[axis] for axis in axes)
    pairs = []
    for i in range(first):
        for j in range(second):
            p, q = source(i, j)
            pairs.append((p * second + q, i * second + j))
    return lax.ppermute(value, axes, pairs)


def gather_plane(own):
    other = shift(own, "z_lo", 1)
    blocks = {}
    for dz, block in ((0, own), (1, other)):
        blocks[0, dz] = block
        for d in (1, 2, 3):
            blocks[d, dz] = shift(block, "x", d)
    return [blocks[key] for key in PLANE]


def gather_wide(own, together=None):
    first = shift(own, "z_lo", 1), shift(own, "x", 1), shift(own, "x", -1)
    if together is not None:
        first, together[:] = lax.optimization_barrier((first, together))
    other, before, after = first
    blocks = {(0, 0): own, (0, 1): other, (1, 0): before, (3, 0): after}
    blocks[1, 1] = shift(other, "x", 1)
    blocks[3, 1] = shift(other, "x", -1)
    blocks[2, 0] = shift(before, "x", 1)
    blocks[2, 1] = shift(blocks[3, 1], "x", -1)
    return [blocks[key] for key in PLANE]


PLANE = [(dx, dz) for dx in range(4) for dz in range(2)]
EARLY, LATE = [0, 1, 2, 6, 7], [3, 4, 5]
STEPS = [(0, 0), (0, 1), (1, 0), (1, 1)]
class Part:
    def __init__(self, table, start):
        self.table, self.start = table, start

    def __getitem__(self, index):
        return self.table[self.start + index]


def call(kernel, outs, scratch=(), vmem=8 << 20, flops=0, start=None, name=None):
    scalars = 0 if start is None else 1

    def body(*refs):
        if scalars:
            refs = (Part(refs[0], start), *refs[1:])
        kernel(*refs)

    def run(*args):
        return pl.pallas_call(
            body,
            out_shape=outs,
            in_specs=[SMEM] * scalars + [VMEM] * (len(args) - scalars),
            out_specs=jax.tree.map(lambda _: VMEM, outs),
            scratch_shapes=list(scratch),
            compiler_params=pltpu.CompilerParams(vmem_limit_bytes=vmem),
            cost_estimate=pl.CostEstimate(flops=flops, bytes_accessed=1 << 20, transcendentals=0),
            name=name,
        )(*args)

    return run


def dot(a, b, dims=((1,), (0,))):
    return lax.dot_general(a, b, (dims, ((), ())), preferred_element_type=F32)


def attend(scale, tokens, table, queries, value_up, *refs):
    blocks, out, scores = refs[:16], refs[16], refs[17]
    rows, _ = queries.shape
    keys = blocks[0].shape[1]
    heads, width, value_width = value_up.shape
    row_pos = table[16] + (lax.broadcasted_iota(jnp.int32, (rows, 1), 0) & (tokens - 1))
    lane = lax.broadcasted_iota(jnp.int32, (1, keys), 1)
    query = queries[...]
    top = jnp.full((rows, 128), NEG, F32)
    for i, block in enumerate(blocks):
        score = dot(query, block[...])
        score = jnp.where(table[i] * keys + lane <= row_pos, score, NEG)
        scores[:, i * keys : (i + 1) * keys] = score
        for j in range(0, keys, 128):
            top = jnp.maximum(top, score[:, j : j + 128])
    top = jnp.max(top, axis=1, keepdims=True)
    total = jnp.zeros((rows, 128), F32)
    added = jnp.zeros((rows, width), F32)
    for i, block in enumerate(blocks):
        raised = jnp.exp((scores[:, i * keys : (i + 1) * keys] - top) * scale)
        for j in range(0, keys, 128):
            total = total + raised[:, j : j + 128]
        added = added + dot(raised.astype(BF16), block[:width, :], ((1,), (1,)))
    context = (added / jnp.sum(total, axis=1, keepdims=True)).astype(BF16)
    for h in range(heads):
        head = dot(context[h * tokens : (h + 1) * tokens], value_up[h])
        out[:, h * value_width : (h + 1) * value_width] = head.astype(BF16)


def project(table, weight, swapped, *refs):
    blocks, outs, rows, sums = refs[:8], refs[8:12], refs[12], refs[13]
    count = blocks[0].shape[0]
    for i, block in enumerate(blocks):
        rows[pl.ds(pl.multiple_of(table[i] * count, count), count), :] = block[...]
    total = rows.shape[0]
    for which, columns in enumerate((weight, swapped)):
        sums[which * total : (which + 1) * total, :] = dot(
            rows[...], columns[...], ((1,), (1,))
        ).astype(BF16)
    quarter = total // 4
    width = outs[0].shape[1] // 2
    for k, out in enumerate(outs):
        for j in range(2):
            at = pl.multiple_of((2 * table[8 + k] + j) * quarter, quarter)
            out[:, j * width : (j + 1) * width] = sums[pl.ds(at, quarter), :]


def add_parts(table, *refs):
    parts, outs = refs[:4], refs[4:8]
    sums = refs[8]
    count, width = outs[0].shape
    total = parts[0][...].astype(F32)
    for part in parts[1:]:
        total = total + part[...].astype(F32)
    for j in range(2):
        sums[2 * j * count : 2 * (j + 1) * count, :] = total[:, j * width : (j + 1) * width]
    for d, out in enumerate(outs):
        at = pl.ds(pl.multiple_of(((table[0] + d) & 3) * count, count), count)
        out[...] = sums[at, :].astype(out.dtype)


def place(table, *refs):
    blocks, outs, choices, rows, routes = refs[:4], refs[4:8], refs[8], refs[9], refs[10]
    count = blocks[0].shape[0]
    width = rows.shape[1] // 2
    picks = (blocks[0].shape[1] - width) // 4
    for k, block in enumerate(blocks):
        at = pl.ds(pl.multiple_of(table[k] * count, count), count)

        @pl.when(table[4 + k] == 0)
        def _(at=at, block=block):
            rows[at, :width] = block[:, :width]
            routes[at, :] = block[:, width:].astype(F32)

        @pl.when(table[4 + k] == 1)
        def _(at=at, block=block):
            rows[at, width:] = block[:, :width]

    total = rows.shape[0]
    index = lax.broadcasted_iota(jnp.int32, (total, total), 0)
    other = lax.broadcasted_iota(jnp.int32, (total, total), 1)
    earlier = (other < index) & (other // count == index // count)
    earlier = jnp.where(earlier, 1.0, 0.0).astype(BF16)
    ids = routes[:, :picks]
    gates = routes[:, picks : 2 * picks] + (
        routes[:, 2 * picks : 3 * picks] + routes[:, 3 * picks :]
    )
    half = lax.broadcasted_iota(jnp.int32, (total, 1), 0) // count
    places = lax.broadcasted_iota(jnp.int32, (total, 2 * CAPACITY), 1).astype(F32)
    for d, out in enumerate(outs):
        match = ids == table[8 + d].astype(F32)
        hit = jnp.max(jnp.where(match, 1.0, 0.0), axis=1, keepdims=True)
        weight = jnp.sum(jnp.where(match, gates, 0.0), axis=1, keepdims=True)
        before = dot(earlier, jnp.broadcast_to(hit, (total, 128)).astype(BF16))[:, :1]
        slot = jnp.where(hit > 0.0, before + (half * CAPACITY).astype(F32), -1.0)
        choices[:, d : d + 1] = slot
        choices[:, 4 + d : 5 + d] = weight
        placing = jnp.where(places == slot, 1.0, 0.0).astype(BF16)
        out[...] = dot(placing, rows[...], ((0,), (0,))).astype(BF16)


def expand(before, table, *refs):
    sums, refs = (refs[0], refs[1:]) if before else (None, refs)
    weights, blocks, out = refs[:4], refs[4:-1], refs[-1]
    hidden = weights[0].shape[2]
    total = sums[...] if before else None
    for i, block in enumerate(blocks):
        weight = jnp.concatenate([weight[table[i]] for weight in weights], axis=1)
        term = dot(block[...], weight)
        total = term if total is None else total + term
    if not before:
        out[...] = total
        return
    for j in range(2):
        gated = total[:, 2 * j * hidden : (2 * j + 1) * hidden]
        upward = total[:, (2 * j + 1) * hidden : (2 * j + 2) * hidden]
        value = gated / (1.0 + jnp.exp(-gated)) * upward
        out[:, j * hidden : (j + 1) * hidden] = value.astype(BF16)


def regroup(table, weight, *outs):
    width = outs[0].shape[2]
    for j in range(8):
        for d, out in enumerate(outs):

            @pl.when(table[j] >> 1 == d)
            def _(j=j, out=out):
                out[table[j] & 1] = weight[:, j * width : (j + 1) * width]


def gather_down(*refs):
    blocks, near, far = refs[:4], refs[4], refs[5]
    for d, block in enumerate(blocks):
        near[d] = block[0]
        far[d] = block[1]


def finish_input(residual, total, *refs):
    parts, routes, out, sent = refs[:3], refs[3], refs[4], refs[5]
    value = residual[...].astype(F32) + total[...]
    for part in parts:
        value = value + part[...].astype(F32)
    width = out.shape[1]
    out[...] = value.astype(BF16)
    sent[:, :width] = value.astype(BF16)
    sent[:, width:] = routes[...]


def contract(near, far, other_near, other_far, *refs):
    blocks, outs = refs[:8], refs[8:]
    total = None
    for i, block in enumerate(blocks):
        own, other = (far, other_far) if i & 1 else (near, other_near)
        term = dot(block[...], jnp.concatenate([own[i >> 1], other[i >> 1]], axis=0))
        total = term if total is None else total + term
    part = outs[0].shape[0]
    for d, out in enumerate(outs):
        out[...] = total[d * part : (d + 1) * part].astype(BF16)


def combine(table, choices, *refs):
    parts, outs, sums = refs[:4], refs[4:8], refs[8]
    total = None
    places = lax.broadcasted_iota(jnp.int32, (choices.shape[0], 2 * CAPACITY), 1).astype(F32)
    for d, block in enumerate(parts):
        weight = jnp.where(places == choices[:, d : d + 1], choices[:, 4 + d : 5 + d], 0.0)
        high = weight.astype(BF16)
        low = (weight - high.astype(F32)).astype(BF16)
        term = dot(high, block[...]) + dot(low, block[...])
        total = term if total is None else total + term
    sums[...] = total
    count, width = outs[0].shape
    for k, out in enumerate(outs):
        at = pl.ds(pl.multiple_of(table[k] * count, count), count)

        @pl.when(table[4 + k] == 0)
        def _(at=at, out=out):
            out[...] = sums[at, :width].astype(BF16)

        @pl.when(table[4 + k] == 1)
        def _(at=at, out=out):
            out[...] = sums[at, width:].astype(BF16)


def struct(*shape, dtype=BF16):
    return jax.ShapeDtypeStruct(shape, dtype)


def tie(value, *others):
    return lax.optimization_barrier((value, *others))[0]


def local(
    queries,
    latents,
    value_up,
    out_proj,
    residual,
    expert_gate,
    expert_up,
    expert_down,
    route_ids,
    route_gates,
):
    tokens, heads, feature_width = queries.shape
    keys = latents.shape[0]
    value_width = value_up.shape[2]
    scale = (value_width + feature_width - value_up.shape[1]) ** (-0.5)
    width = out_proj.shape[1]
    x, z, core = (lax.axis_index(axis) for axis in CTX)
    plane, row = (lax.axis_index(axis) for axis in EP)
    chips = [(((x - dx) & 3), (z ^ dz)) for dx, dz in PLANE]
    owners = [cx * 4 + cz * 2 + (core ^ dk) for dk in range(2) for cx, cz in chips]
    me = x * 4 + z * 2 + core

    first = keys * 16 - tokens * 16 + me * tokens
    b_k = [(plane & 1) ^ k0 for _, k0 in STEPS] + [(plane >> 1) ^ k1 for k1, _ in STEPS]
    entries = {
        "regroup": [(((j >> 1) - x) & 3) * 2 + (z ^ (j & 1)) for j in range(8)],
        "attend": owners + [first],
        "project": [cz * 4 + cx for cx, cz in chips]
        + [((row & 1) ^ k0 ^ core) * 2 + ((row >> 1) ^ k1) for k1, k0 in STEPS],
        "add_parts": [plane],
        "place": b_k + [plane * 4 + ((row + d) & 3) for d in range(4)],
        "early": [chips[i][0] * 2 + chips[i][1] for i in EARLY],
        "late": [chips[i][0] * 2 + chips[i][1] for i in LATE],
    }
    starts, table = {}, []
    for name, values in entries.items():
        starts[name] = len(table)
        table += values
    table = jnp.stack(table).astype(jnp.int32)

    rows = jnp.transpose(queries, (1, 0, 2)).reshape(heads * tokens, feature_width)
    gathered = gather_wide(jnp.transpose(latents), [])
    hidden_width = expert_gate.shape[2]
    down = call(
        regroup,
        [struct(2, hidden_width, 2 * width)] * 4,
        start=starts["regroup"],
        name="regroup",
    )(table, expert_down[0])
    down = list(down)
    gathered[6], rows, down[0] = lax.optimization_barrier((gathered[6], rows, down[0]))
    swapped = [shift(block, "core", 1) for block in gathered]
    out_weight = jnp.transpose(out_proj)
    out_swapped = shift(tie(out_weight, *gathered), "core", 1)
    gates = []
    rest = route_gates
    for _ in range(3):
        gates.append(rest.astype(BF16))
        rest = rest - gates[-1].astype(F32)
    routes = jnp.concatenate([route_ids.astype(BF16), *gates], axis=1)

    down[1] = shift(tie(down[1], *gathered), "x", 1)
    down[3] = shift(tie(down[3], *gathered), "x", 3)
    head_out = call(
        functools.partial(attend, scale, tokens),
        struct(tokens, heads * value_width),
        [pltpu.VMEM((heads * tokens, 16 * keys), F32)],
        vmem=20 << 20,
        flops=10 << 30,
        start=starts["attend"],
        name="attend",
    )(table, rows, value_up, *gathered, *swapped)

    head_out, out_swapped, down[1], down[3] = lax.optimization_barrier(
        (head_out, out_swapped, down[1], down[3])
    )

    count = route_ids.shape[0]

    gathered_heads = gather_plane(head_out)
    parts = call(
        project,
        [struct(2 * tokens, 2 * width)] * 4,
        [
            pltpu.VMEM((8 * tokens, heads * value_width), BF16),
            pltpu.VMEM((16 * tokens, width), BF16),
        ],
        vmem=16 << 20,
        flops=2 << 30,
        start=starts["project"],
        name="project",
    )(
        table,
        out_weight,
        out_swapped,
        *gathered_heads,
    )
    down[2] = shift(tie(down[2], parts[0]), "x", 2)
    parts = [
        permute(part, ("core", "y"), lambda c, y: (y & 1, ((y >> 1) ^ k1) * 2 + (c ^ k0)))
        for part, (k1, k0) in zip(parts, STEPS)
    ]
    sums = call(
        add_parts,
        [struct(count, width, dtype=F32)] + [struct(count, width)] * 3,
        [pltpu.VMEM((4 * count, width), F32)],
        start=starts["add_parts"],
        name="add_parts",
    )(table, *parts)
    down[2], *sums = lax.optimization_barrier((down[2], *sums))
    near, far = call(
        gather_down, [struct(4, hidden_width, 2 * width)] * 2, name="gather_down"
    )(*down)
    moe_input, routed_input = call(
        finish_input,
        [struct(count, width), struct(count, width + routes.shape[1])],
        name="finish_input",
    )(residual, sums[0], *[shift(sums[d], "z_hi", d) for d in (1, 2, 3)], routes)
    routed_input, near, far = lax.optimization_barrier((routed_input, near, far))

    planes = [
        permute(
            routed_input,
            ("core", "z_hi"),
            lambda c, p: ((p >> 1) ^ k1, 2 * c + ((p & 1) ^ k0)),
        )
        for k1, k0 in STEPS
    ]
    *outgoing, choices = call(
        place,
        [struct(2 * CAPACITY, 2 * width)] * 4 + [struct(2 * count, 8, dtype=F32)],
        [pltpu.VMEM((2 * count, 2 * width), BF16), pltpu.VMEM((2 * count, routes.shape[1]), F32)],
        start=starts["place"],
        name="place",
    )(table, *planes)
    arrived = [outgoing[0]] + [shift(outgoing[d], "y", d) for d in (1, 2, 3)]
    arrived = jnp.concatenate(arrived, axis=0)
    gate, up, near = lax.optimization_barrier((expert_gate, expert_up, near, arrived))[:3]
    gate = gate.reshape(8, 2 * width, hidden_width)
    up = up.reshape(8, 2 * width, hidden_width)
    swapped = [shift(gate, "core", 1), shift(up, "core", 1)]
    slots = gather_wide(arrived, swapped)
    gate_swapped, up_swapped = swapped
    far = shift(tie(far, slots[1]), "z_lo", 1)
    near_swapped = shift(tie(near, slots[1]), "core", 1)

    weights = (gate, up, gate_swapped, up_swapped)
    part = struct(8 * CAPACITY, 4 * hidden_width, dtype=F32)
    hidden = ()
    last = struct(8 * CAPACITY, 2 * hidden_width)
    for name, some, out in (("early", EARLY, part), ("late", LATE, last)):
        hidden = call(
            functools.partial(expand, len(hidden)),
            out,
            vmem=16 << 20,
            flops=len(some) * (512 << 20),
            start=starts[name],
            name="expand",
        )(table, *hidden, *weights, *[slots[i] for i in some])
        hidden = (hidden,)
    (hidden,) = hidden
    hidden, near_swapped, far = lax.optimization_barrier((hidden, near_swapped, far))
    far_swapped = shift(far, "core", 1)
    hidden = gather_plane(hidden)
    results = call(
        contract,
        [struct(2 * CAPACITY, 2 * width)] * 4,
        vmem=16 << 20,
        flops=2 << 30,
        name="contract",
    )(near, far, near_swapped, far_swapped, *hidden)

    returned = [results[0]] + [shift(results[d], "y", -d) for d in (1, 2, 3)]
    sums = call(
        combine,
        [struct(count, width)] * 4,
        [pltpu.VMEM((2 * count, 2 * width), F32)],
        start=starts["place"],
        name="combine",
    )(table, choices, *returned)
    routed = None
    for part, (k1, k0) in zip(sums, STEPS):
        part = permute(
            part,
            ("core", "z_hi"),
            lambda c, p: (p >> 1, ((c ^ k1) << 1) | ((p & 1) ^ k0)),
        ).astype(F32)
        routed = part if routed is None else routed + part
    return (moe_input.astype(F32) + routed).astype(BF16)


def solution(mesh):
    split = Mesh(mesh.devices.reshape(tuple(SIZES.values())), tuple(SIZES))
    return jax.shard_map(
        local,
        mesh=split,
        in_specs=(
            P(CTX, EP, None),
            P(CTX, None),
            P(EP, None, None),
            P(EP, CTX),
            P(EP, CTX),
            P(EP, None, CTX),
            P(EP, None, CTX),
            P(EP, CTX, None),
            P(EP, None),
            P(EP, None),
        ),
        out_specs=P(EP, CTX),
        check_vma=False,
    )
```

```python
import functools

import jax
import jax.numpy as jnp
from jax import lax
from jax.experimental import pallas as pl
from jax.experimental.pallas import tpu as pltpu
from jax.sharding import Mesh
from jax.sharding import PartitionSpec as P

NEG = -1e30
CTX = ("x", "z_lo", "core")
EP = ("z_hi", "y")
SIZES = {"x": 4, "z_lo": 2, "core": 2, "z_hi": 4, "y": 4}
CAPACITY = 36
F32, BF16 = jnp.float32, jnp.bfloat16
VMEM = pl.BlockSpec(memory_space=pltpu.VMEM)
SMEM = pl.BlockSpec(memory_space=pltpu.SMEM)


def shift(value, axis, by):
    size = SIZES[axis]
    return lax.ppermute(value, axis, [(i, (i + by) % size) for i in range(size)])


def permute(value, axes, source):
    first, second = (SIZES[axis] for axis in axes)
    pairs = []
    for i in range(first):
        for j in range(second):
            p, q = source(i, j)
            pairs.append((p * second + q, i * second + j))
    return lax.ppermute(value, axes, pairs)


def gather_plane(own):
    other = shift(own, "z_lo", 1)
    blocks = {}
    for dz, block in ((0, own), (1, other)):
        blocks[0, dz] = block
        for d in (1, 2, 3):
            blocks[d, dz] = shift(block, "x", d)
    return [blocks[key] for key in PLANE]


def gather_wide(own, together=None):
    first = shift(own, "z_lo", 1), shift(own, "x", 1), shift(own, "x", -1)
    if together is not None:
        first, together[:] = lax.optimization_barrier((first, together))
    other, before, after = first
    blocks = {(0, 0): own, (0, 1): other, (1, 0): before, (3, 0): after}
    blocks[1, 1] = shift(other, "x", 1)
    blocks[3, 1] = shift(other, "x", -1)
    blocks[2, 0] = shift(before, "x", 1)
    blocks[2, 1] = shift(blocks[3, 1], "x", -1)
    return [blocks[key] for key in PLANE]


PLANE = [(dx, dz) for dx in range(4) for dz in range(2)]
EARLY, LATE = [0, 1, 2, 6, 7], [3, 4, 5]
STEPS = [(0, 0), (0, 1), (1, 0), (1, 1)]
class Part:
    def __init__(self, table, start):
        self.table, self.start = table, start

    def __getitem__(self, index):
        return self.table[self.start + index]


def call(kernel, outs, scratch=(), vmem=8 << 20, flops=0, start=None, name=None):
    scalars = 0 if start is None else 1

    def body(*refs):
        if scalars:
            refs = (Part(refs[0], start), *refs[1:])
        kernel(*refs)

    def run(*args):
        return pl.pallas_call(
            body,
            out_shape=outs,
            in_specs=[SMEM] * scalars + [VMEM] * (len(args) - scalars),
            out_specs=jax.tree.map(lambda _: VMEM, outs),
            scratch_shapes=list(scratch),
            compiler_params=pltpu.CompilerParams(vmem_limit_bytes=vmem),
            cost_estimate=pl.CostEstimate(flops=flops, bytes_accessed=1 << 20, transcendentals=0),
            name=name,
        )(*args)

    return run


def dot(a, b, dims=((1,), (0,))):
    return lax.dot_general(a, b, (dims, ((), ())), preferred_element_type=F32)


def attend(scale, tokens, table, queries, value_up, *refs):
    blocks, out, scores = refs[:16], refs[16], refs[17]
    rows, _ = queries.shape
    keys = blocks[0].shape[1]
    heads, width, value_width = value_up.shape
    row_pos = table[16] + (lax.broadcasted_iota(jnp.int32, (rows, 1), 0) & (tokens - 1))
    lane = lax.broadcasted_iota(jnp.int32, (1, keys), 1)
    query = queries[...]
    top = jnp.full((rows, 128), NEG, F32)
    for i, block in enumerate(blocks):
        score = dot(query, block[...])
        score = jnp.where(table[i] * keys + lane <= row_pos, score, NEG)
        scores[:, i * keys : (i + 1) * keys] = score
        for j in range(0, keys, 128):
            top = jnp.maximum(top, score[:, j : j + 128])
    top = jnp.max(top, axis=1, keepdims=True)
    total = jnp.zeros((rows, 128), F32)
    added = jnp.zeros((rows, width), F32)
    for i, block in enumerate(blocks):
        raised = jnp.exp((scores[:, i * keys : (i + 1) * keys] - top) * scale)
        for j in range(0, keys, 128):
            total = total + raised[:, j : j + 128]
        added = added + dot(raised.astype(BF16), block[:width, :], ((1,), (1,)))
    context = (added / jnp.sum(total, axis=1, keepdims=True)).astype(BF16)
    for h in range(heads):
        head = dot(context[h * tokens : (h + 1) * tokens], value_up[h])
        out[:, h * value_width : (h + 1) * value_width] = head.astype(BF16)


def project(table, weight, swapped, *refs):
    blocks, outs, rows, sums = refs[:8], refs[8:12], refs[12], refs[13]
    count = blocks[0].shape[0]
    for i, block in enumerate(blocks):
        rows[pl.ds(pl.multiple_of(table[i] * count, count), count), :] = block[...]
    total = rows.shape[0]
    for which, columns in enumerate((weight, swapped)):
        sums[which * total : (which + 1) * total, :] = dot(
            rows[...], columns[...], ((1,), (1,))
        ).astype(BF16)
    quarter = total // 4
    width = outs[0].shape[1] // 2
    for k, out in enumerate(outs):
        for j in range(2):
            at = pl.multiple_of((2 * table[8 + k] + j) * quarter, quarter)
            out[:, j * width : (j + 1) * width] = sums[pl.ds(at, quarter), :]


def add_parts(table, *refs):
    parts, outs = refs[:4], refs[4:8]
    sums = refs[8]
    count, width = outs[0].shape
    total = parts[0][...].astype(F32)
    for part in parts[1:]:
        total = total + part[...].astype(F32)
    for j in range(2):
        sums[2 * j * count : 2 * (j + 1) * count, :] = total[:, j * width : (j + 1) * width]
    for d, out in enumerate(outs):
        at = pl.ds(pl.multiple_of(((table[0] + d) & 3) * count, count), count)
        out[...] = sums[at, :].astype(out.dtype)


def join(table, own, other, out):
    width = (out.shape[1] - 32) // 2
    for core, (first, second) in enumerate(((own, other), (other, own))):

        @pl.when(table[0] == core)
        def _(first=first, second=second):
            out[:, :width] = first[:, :width]
            out[:, width : 2 * width] = second[:, :width]

    out[:, 2 * width :] = own[:, width:]


def place(table, *refs):
    blocks, outs, choices, rows, routes = refs[:2], refs[2:6], refs[6], refs[7], refs[8]
    count = blocks[0].shape[0]
    width = rows.shape[1]
    picks = (blocks[0].shape[1] - width) // 4
    for k, block in enumerate(blocks):
        at = pl.ds(pl.multiple_of(table[k] * count, count), count)
        rows[at, :] = block[:, :width]
        routes[at, :] = block[:, width:].astype(F32)

    total = rows.shape[0]
    index = lax.broadcasted_iota(jnp.int32, (total, total), 0)
    other = lax.broadcasted_iota(jnp.int32, (total, total), 1)
    earlier = (other < index) & (other // count == index // count)
    earlier = jnp.where(earlier, 1.0, 0.0).astype(BF16)
    ids = routes[:, :picks]
    gates = routes[:, picks : 2 * picks] + (
        routes[:, 2 * picks : 3 * picks] + routes[:, 3 * picks :]
    )
    half = lax.broadcasted_iota(jnp.int32, (total, 1), 0) // count
    places = lax.broadcasted_iota(jnp.int32, (total, 2 * CAPACITY), 1).astype(F32)
    for d, out in enumerate(outs):
        match = ids == table[2 + d].astype(F32)
        hit = jnp.max(jnp.where(match, 1.0, 0.0), axis=1, keepdims=True)
        weight = jnp.sum(jnp.where(match, gates, 0.0), axis=1, keepdims=True)
        before = dot(earlier, jnp.broadcast_to(hit, (total, 128)).astype(BF16))[:, :1]
        slot = jnp.where(hit > 0.0, before + (half * CAPACITY).astype(F32), -1.0)
        choices[:, d : d + 1] = slot
        choices[:, 4 + d : 5 + d] = weight
        placing = jnp.where(places == slot, 1.0, 0.0).astype(BF16)
        out[...] = dot(placing, rows[...], ((0,), (0,))).astype(BF16)


def expand(before, table, *refs):
    sums, refs = (refs[0], refs[1:]) if before else (None, refs)
    weights, blocks, out = refs[:4], refs[4:-1], refs[-1]
    hidden = weights[0].shape[2]
    total = sums[...] if before else None
    for i, block in enumerate(blocks):
        weight = jnp.concatenate([weight[table[i]] for weight in weights], axis=1)
        term = dot(block[...], weight)
        total = term if total is None else total + term
    if not before:
        out[...] = total
        return
    for j in range(2):
        gated = total[:, 2 * j * hidden : (2 * j + 1) * hidden]
        upward = total[:, (2 * j + 1) * hidden : (2 * j + 2) * hidden]
        value = gated / (1.0 + jnp.exp(-gated)) * upward
        out[:, j * hidden : (j + 1) * hidden] = value.astype(BF16)


def regroup(table, weight, *outs):
    width = outs[0].shape[2]
    for j in range(8):
        for d, out in enumerate(outs):

            @pl.when(table[j] >> 1 == d)
            def _(j=j, out=out):
                out[table[j] & 1] = weight[:, j * width : (j + 1) * width]


def gather_down(*refs):
    blocks, near, far = refs[:4], refs[4], refs[5]
    for d, block in enumerate(blocks):
        near[d] = block[0]
        far[d] = block[1]


def finish_input(residual, total, *refs):
    parts, routes, out, sent = refs[:3], refs[3], refs[4], refs[5]
    value = residual[...].astype(F32) + total[...]
    for part in parts:
        value = value + part[...].astype(F32)
    width = out.shape[1]
    out[...] = value.astype(BF16)
    sent[:, :width] = value.astype(BF16)
    sent[:, width:] = routes[...]


def contract(near, far, other_near, other_far, *refs):
    blocks, outs = refs[:8], refs[8:]
    total = None
    for i, block in enumerate(blocks):
        own, other = (far, other_far) if i & 1 else (near, other_near)
        term = dot(block[...], jnp.concatenate([own[i >> 1], other[i >> 1]], axis=0))
        total = term if total is None else total + term
    part = outs[0].shape[0]
    for d, out in enumerate(outs):
        out[...] = total[d * part : (d + 1) * part].astype(BF16)


def combine(table, choices, *refs):
    parts, outs, sums = refs[:4], refs[4:8], refs[8]
    total = None
    places = lax.broadcasted_iota(jnp.int32, (choices.shape[0], 2 * CAPACITY), 1).astype(F32)
    for d, block in enumerate(parts):
        weight = jnp.where(places == choices[:, d : d + 1], choices[:, 4 + d : 5 + d], 0.0)
        high = weight.astype(BF16)
        low = (weight - high.astype(F32)).astype(BF16)
        term = dot(high, block[...]) + dot(low, block[...])
        total = term if total is None else total + term
    sums[...] = total
    count, width = outs[0].shape
    for k, out in enumerate(outs):
        at = pl.ds(pl.multiple_of(table[k] * count, count), count)

        @pl.when(table[4 + k] == 0)
        def _(at=at, out=out):
            out[...] = sums[at, :width].astype(BF16)

        @pl.when(table[4 + k] == 1)
        def _(at=at, out=out):
            out[...] = sums[at, width:].astype(BF16)


def struct(*shape, dtype=BF16):
    return jax.ShapeDtypeStruct(shape, dtype)


def tie(value, *others):
    return lax.optimization_barrier((value, *others))[0]


def local(
    queries,
    latents,
    value_up,
    out_proj,
    residual,
    expert_gate,
    expert_up,
    expert_down,
    route_ids,
    route_gates,
):
    tokens, heads, feature_width = queries.shape
    keys = latents.shape[0]
    value_width = value_up.shape[2]
    scale = (value_width + feature_width - value_up.shape[1]) ** (-0.5)
    width = out_proj.shape[1]
    x, z, core = (lax.axis_index(axis) for axis in CTX)
    plane, row = (lax.axis_index(axis) for axis in EP)
    chips = [(((x - dx) & 3), (z ^ dz)) for dx, dz in PLANE]
    owners = [cx * 4 + cz * 2 + (core ^ dk) for dk in range(2) for cx, cz in chips]
    me = x * 4 + z * 2 + core

    first = keys * 16 - tokens * 16 + me * tokens
    b_k = [(plane & 1) ^ k0 for _, k0 in STEPS] + [(plane >> 1) ^ k1 for k1, _ in STEPS]
    entries = {
        "regroup": [(((j >> 1) - x) & 3) * 2 + (z ^ (j & 1)) for j in range(8)],
        "attend": owners + [first],
        "project": [cz * 4 + cx for cx, cz in chips]
        + [((row & 1) ^ k0 ^ core) * 2 + ((row >> 1) ^ k1) for k1, k0 in STEPS],
        "add_parts": [plane],
        "join": [core],
        "combine": b_k,
        "place": [(plane & 1) ^ k0 for k0 in (0, 1)] + [plane * 4 + ((row + d) & 3) for d in range(4)],
        "early": [chips[i][0] * 2 + chips[i][1] for i in EARLY],
        "late": [chips[i][0] * 2 + chips[i][1] for i in LATE],
    }
    starts, table = {}, []
    for name, values in entries.items():
        starts[name] = len(table)
        table += values
    table = jnp.stack(table).astype(jnp.int32)

    rows = jnp.transpose(queries, (1, 0, 2)).reshape(heads * tokens, feature_width)
    gathered = gather_wide(jnp.transpose(latents), [])
    hidden_width = expert_gate.shape[2]
    down = call(
        regroup,
        [struct(2, hidden_width, 2 * width)] * 4,
        start=starts["regroup"],
        name="regroup",
    )(table, expert_down[0])
    down = list(down)
    gathered[6], rows, down[0] = lax.optimization_barrier((gathered[6], rows, down[0]))
    swapped = [shift(block, "core", 1) for block in gathered]
    out_weight = jnp.transpose(out_proj)
    out_swapped = shift(tie(out_weight, *gathered), "core", 1)
    gates = []
    rest = route_gates
    for _ in range(3):
        gates.append(rest.astype(BF16))
        rest = rest - gates[-1].astype(F32)
    routes = jnp.concatenate([route_ids.astype(BF16), *gates], axis=1)

    down[1] = shift(tie(down[1], *gathered), "x", 1)
    down[3] = shift(tie(down[3], *gathered), "x", 3)
    head_out = call(
        functools.partial(attend, scale, tokens),
        struct(tokens, heads * value_width),
        [pltpu.VMEM((heads * tokens, 16 * keys), F32)],
        vmem=20 << 20,
        flops=10 << 30,
        start=starts["attend"],
        name="attend",
    )(table, rows, value_up, *gathered, *swapped)

    head_out, out_swapped, down[1], down[3] = lax.optimization_barrier(
        (head_out, out_swapped, down[1], down[3])
    )

    count = route_ids.shape[0]

    gathered_heads = gather_plane(head_out)
    parts = call(
        project,
        [struct(2 * tokens, 2 * width)] * 4,
        [
            pltpu.VMEM((8 * tokens, heads * value_width), BF16),
            pltpu.VMEM((16 * tokens, width), BF16),
        ],
        vmem=16 << 20,
        flops=2 << 30,
        start=starts["project"],
        name="project",
    )(
        table,
        out_weight,
        out_swapped,
        *gathered_heads,
    )
    down[2] = shift(tie(down[2], parts[0]), "x", 2)
    parts = [
        permute(part, ("core", "y"), lambda c, y: (y & 1, ((y >> 1) ^ k1) * 2 + (c ^ k0)))
        for part, (k1, k0) in zip(parts, STEPS)
    ]
    sums = call(
        add_parts,
        [struct(count, width, dtype=F32)] + [struct(count, width)] * 3,
        [pltpu.VMEM((4 * count, width), F32)],
        start=starts["add_parts"],
        name="add_parts",
    )(table, *parts)
    down[2], *sums = lax.optimization_barrier((down[2], *sums))
    near, far = call(
        gather_down, [struct(4, hidden_width, 2 * width)] * 2, name="gather_down"
    )(*down)
    moe_input, routed_input = call(
        finish_input,
        [struct(count, width), struct(count, width + routes.shape[1])],
        name="finish_input",
    )(residual, sums[0], *[shift(sums[d], "z_hi", d) for d in (1, 2, 3)], routes)
    routed_input, near, far = lax.optimization_barrier((routed_input, near, far))

    joined = call(
        join, struct(count, 2 * width + routes.shape[1]), start=starts["join"], name="join"
    )(table, routed_input, shift(routed_input, "core", 1))
    planes = [
        permute(joined, ("core", "z_hi"), lambda c, p: (p >> 1, 2 * c + (k0 ^ (p & 1))))
        for k0 in (0, 1)
    ]
    *outgoing, choices = call(
        place,
        [struct(2 * CAPACITY, 2 * width)] * 4 + [struct(2 * count, 8, dtype=F32)],
        [pltpu.VMEM((2 * count, 2 * width), BF16), pltpu.VMEM((2 * count, routes.shape[1]), F32)],
        start=starts["place"],
        name="place",
    )(table, *planes)
    arrived = [outgoing[0]] + [shift(outgoing[d], "y", d) for d in (1, 2, 3)]
    arrived = jnp.concatenate(arrived, axis=0)
    gate, up, near = lax.optimization_barrier((expert_gate, expert_up, near, arrived))[:3]
    gate = gate.reshape(8, 2 * width, hidden_width)
    up = up.reshape(8, 2 * width, hidden_width)
    swapped = [shift(gate, "core", 1), shift(up, "core", 1)]
    slots = gather_wide(arrived, swapped)
    gate_swapped, up_swapped = swapped
    far = shift(tie(far, slots[1]), "z_lo", 1)
    near_swapped = shift(tie(near, slots[1]), "core", 1)

    weights = (gate, up, gate_swapped, up_swapped)
    part = struct(8 * CAPACITY, 4 * hidden_width, dtype=F32)
    hidden = ()
    last = struct(8 * CAPACITY, 2 * hidden_width)
    for name, some, out in (("early", EARLY, part), ("late", LATE, last)):
        hidden = call(
            functools.partial(expand, len(hidden)),
            out,
            vmem=16 << 20,
            flops=len(some) * (512 << 20),
            start=starts[name],
            name="expand",
        )(table, *hidden, *weights, *[slots[i] for i in some])
        hidden = (hidden,)
    (hidden,) = hidden
    hidden, near_swapped, far = lax.optimization_barrier((hidden, near_swapped, far))
    far_swapped = shift(far, "core", 1)
    hidden = gather_plane(hidden)
    results = call(
        contract,
        [struct(2 * CAPACITY, 2 * width)] * 4,
        vmem=16 << 20,
        flops=2 << 30,
        name="contract",
    )(near, far, near_swapped, far_swapped, *hidden)

    returned = [results[0]] + [shift(results[d], "y", -d) for d in (1, 2, 3)]
    sums = call(
        combine,
        [struct(count, width)] * 4,
        [pltpu.VMEM((2 * count, 2 * width), F32)],
        start=starts["combine"],
        name="combine",
    )(table, choices, *returned)
    routed = None
    for part, (k1, k0) in zip(sums, STEPS):
        part = permute(
            part,
            ("core", "z_hi"),
            lambda c, p: (p >> 1, ((c ^ k1) << 1) | ((p & 1) ^ k0)),
        ).astype(F32)
        routed = part if routed is None else routed + part
    return (moe_input.astype(F32) + routed).astype(BF16)


def solution(mesh):
    split = Mesh(mesh.devices.reshape(tuple(SIZES.values())), tuple(SIZES))
    return jax.shard_map(
        local,
        mesh=split,
        in_specs=(
            P(CTX, EP, None),
            P(CTX, None),
            P(EP, None, None),
            P(EP, CTX),
            P(EP, CTX),
            P(EP, None, CTX),
            P(EP, None, CTX),
            P(EP, CTX, None),
            P(EP, None),
            P(EP, None),
        ),
        out_specs=P(EP, CTX),
        check_vma=False,
    )
```

```python
import functools

import jax
import jax.numpy as jnp
from jax import lax
from jax.experimental import pallas as pl
from jax.experimental.pallas import tpu as pltpu
from jax.sharding import Mesh
from jax.sharding import PartitionSpec as P

NEG = -1e30
CTX = ("x", "z_lo", "core")
EP = ("z_hi", "y")
SIZES = {"x": 4, "z_lo": 2, "core": 2, "z_hi": 4, "y": 4}
CAPACITY = 36
F32, BF16 = jnp.float32, jnp.bfloat16
VMEM = pl.BlockSpec(memory_space=pltpu.VMEM)
SMEM = pl.BlockSpec(memory_space=pltpu.SMEM)


def shift(value, axis, by):
    size = SIZES[axis]
    return lax.ppermute(value, axis, [(i, (i + by) % size) for i in range(size)])


def permute(value, axes, source):
    first, second = (SIZES[axis] for axis in axes)
    pairs = []
    for i in range(first):
        for j in range(second):
            p, q = source(i, j)
            pairs.append((p * second + q, i * second + j))
    return lax.ppermute(value, axes, pairs)


def gather_plane(own):
    other = shift(own, "z_lo", 1)
    blocks = {}
    for dz, block in ((0, own), (1, other)):
        blocks[0, dz] = block
        for d in (1, 2, 3):
            blocks[d, dz] = shift(block, "x", d)
    return [blocks[key] for key in PLANE]


def gather_wide(own, together=None):
    first = shift(own, "z_lo", 1), shift(own, "x", 1), shift(own, "x", -1)
    if together is not None:
        first, together[:] = lax.optimization_barrier((first, together))
    other, before, after = first
    blocks = {(0, 0): own, (0, 1): other, (1, 0): before, (3, 0): after}
    blocks[1, 1] = shift(other, "x", 1)
    blocks[3, 1] = shift(other, "x", -1)
    blocks[2, 0] = shift(before, "x", 1)
    blocks[2, 1] = shift(blocks[3, 1], "x", -1)
    return [blocks[key] for key in PLANE]


PLANE = [(dx, dz) for dx in range(4) for dz in range(2)]
EARLY, LATE = [0, 1, 2, 6, 7], [3, 4, 5]
STEPS = [(0, 0), (0, 1), (1, 0), (1, 1)]
class Part:
    def __init__(self, table, start):
        self.table, self.start = table, start

    def __getitem__(self, index):
        return self.table[self.start + index]


def call(kernel, outs, scratch=(), vmem=8 << 20, flops=0, start=None, name=None):
    scalars = 0 if start is None else 1

    def body(*refs):
        if scalars:
            refs = (Part(refs[0], start), *refs[1:])
        kernel(*refs)

    def run(*args):
        return pl.pallas_call(
            body,
            out_shape=outs,
            in_specs=[SMEM] * scalars + [VMEM] * (len(args) - scalars),
            out_specs=jax.tree.map(lambda _: VMEM, outs),
            scratch_shapes=list(scratch),
            compiler_params=pltpu.CompilerParams(vmem_limit_bytes=vmem),
            cost_estimate=pl.CostEstimate(flops=flops, bytes_accessed=1 << 20, transcendentals=0),
            name=name,
        )(*args)

    return run


def dot(a, b, dims=((1,), (0,))):
    return lax.dot_general(a, b, (dims, ((), ())), preferred_element_type=F32)


def attend(scale, tokens, table, queries, value_up, *refs):
    blocks, out, scores = refs[:16], refs[16], refs[17]
    rows, _ = queries.shape
    keys = blocks[0].shape[1]
    heads, width, value_width = value_up.shape
    row_pos = table[16] + (lax.broadcasted_iota(jnp.int32, (rows, 1), 0) & (tokens - 1))
    lane = lax.broadcasted_iota(jnp.int32, (1, keys), 1)
    query = queries[...]
    top = jnp.full((rows, 128), NEG, F32)
    for i, block in enumerate(blocks):
        score = dot(query, block[...])
        score = jnp.where(table[i] * keys + lane <= row_pos, score, NEG)
        scores[:, i * keys : (i + 1) * keys] = score
        for j in range(0, keys, 128):
            top = jnp.maximum(top, score[:, j : j + 128])
    top = jnp.max(top, axis=1, keepdims=True)
    total = jnp.zeros((rows, 128), F32)
    added = jnp.zeros((rows, width), F32)
    for i, block in enumerate(blocks):
        raised = jnp.exp((scores[:, i * keys : (i + 1) * keys] - top) * scale)
        for j in range(0, keys, 128):
            total = total + raised[:, j : j + 128]
        added = added + dot(raised.astype(BF16), block[:width, :], ((1,), (1,)))
    context = (added / jnp.sum(total, axis=1, keepdims=True)).astype(BF16)
    for h in range(heads):
        head = dot(context[h * tokens : (h + 1) * tokens], value_up[h])
        out[:, h * value_width : (h + 1) * value_width] = head.astype(BF16)


def project(table, weight, swapped, *refs):
    blocks, outs, rows, sums = refs[:8], refs[8:12], refs[12], refs[13]
    count = blocks[0].shape[0]
    for i, block in enumerate(blocks):
        rows[pl.ds(pl.multiple_of(table[i] * count, count), count), :] = block[...]
    total = rows.shape[0]
    for which, columns in enumerate((weight, swapped)):
        sums[which * total : (which + 1) * total, :] = dot(
            rows[...], columns[...], ((1,), (1,))
        ).astype(BF16)
    quarter = total // 4
    width = outs[0].shape[1] // 2
    for k, out in enumerate(outs):
        for j in range(2):
            at = pl.multiple_of((2 * table[8 + k] + j) * quarter, quarter)
            out[:, j * width : (j + 1) * width] = sums[pl.ds(at, quarter), :]


def add_parts(table, *refs):
    parts, kept, sent, sums = refs[:4], refs[4], refs[5], refs[6]
    count = kept.shape[0]
    width = kept.shape[1]
    total = parts[0][...].astype(F32)
    for part in parts[1:]:
        total = total + part[...].astype(F32)
    for j in range(2):
        sums[j * count : (j + 1) * count, :] = total[:, j * width : (j + 1) * width]
    mine = pl.multiple_of((table[0] >> 1) * count, count)
    kept[...] = sums[pl.ds(mine, count), :]
    sent[...] = sums[pl.ds(count - mine, count), :].astype(BF16)


def add_pair(table, kept, part, own, sent, sums):
    count = own.shape[0]
    sums[...] = kept[...] + part[...].astype(F32)
    mine = pl.multiple_of((table[0] & 1) * count, count)
    own[...] = sums[pl.ds(mine, count), :]
    sent[...] = sums[pl.ds(count - mine, count), :].astype(BF16)


def join(table, own, other, out):
    width = (out.shape[1] - 32) // 2
    for core, (first, second) in enumerate(((own, other), (other, own))):

        @pl.when(table[0] == core)
        def _(first=first, second=second):
            out[:, :width] = first[:, :width]
            out[:, width : 2 * width] = second[:, :width]

    out[:, 2 * width :] = own[:, width:]


def place(table, *refs):
    blocks, outs, choices, rows, routes = refs[:2], refs[2:6], refs[6], refs[7], refs[8]
    count = blocks[0].shape[0]
    width = rows.shape[1]
    picks = (blocks[0].shape[1] - width) // 4
    for k, block in enumerate(blocks):
        at = pl.ds(pl.multiple_of(table[k] * count, count), count)
        rows[at, :] = block[:, :width]
        routes[at, :] = block[:, width:].astype(F32)

    total = rows.shape[0]
    index = lax.broadcasted_iota(jnp.int32, (total, total), 0)
    other = lax.broadcasted_iota(jnp.int32, (total, total), 1)
    earlier = (other < index) & (other // count == index // count)
    earlier = jnp.where(earlier, 1.0, 0.0).astype(BF16)
    ids = routes[:, :picks]
    gates = routes[:, picks : 2 * picks] + (
        routes[:, 2 * picks : 3 * picks] + routes[:, 3 * picks :]
    )
    half = lax.broadcasted_iota(jnp.int32, (total, 1), 0) // count
    places = lax.broadcasted_iota(jnp.int32, (total, 2 * CAPACITY), 1).astype(F32)
    for d, out in enumerate(outs):
        match = ids == table[2 + d].astype(F32)
        hit = jnp.max(jnp.where(match, 1.0, 0.0), axis=1, keepdims=True)
        weight = jnp.sum(jnp.where(match, gates, 0.0), axis=1, keepdims=True)
        before = dot(earlier, jnp.broadcast_to(hit, (total, 128)).astype(BF16))[:, :1]
        slot = jnp.where(hit > 0.0, before + (half * CAPACITY).astype(F32), -1.0)
        choices[:, d : d + 1] = slot
        choices[:, 4 + d : 5 + d] = weight
        placing = jnp.where(places == slot, 1.0, 0.0).astype(BF16)
        out[...] = dot(placing, rows[...], ((0,), (0,))).astype(BF16)


def expand(before, table, *refs):
    sums, refs = (refs[0], refs[1:]) if before else (None, refs)
    weights, blocks, out = refs[:4], refs[4:-1], refs[-1]
    hidden = weights[0].shape[2]
    total = sums[...] if before else None
    for i, block in enumerate(blocks):
        weight = jnp.concatenate([weight[table[i]] for weight in weights], axis=1)
        term = dot(block[...], weight)
        total = term if total is None else total + term
    if not before:
        out[...] = total
        return
    for j in range(2):
        gated = total[:, 2 * j * hidden : (2 * j + 1) * hidden]
        upward = total[:, (2 * j + 1) * hidden : (2 * j + 2) * hidden]
        value = gated / (1.0 + jnp.exp(-gated)) * upward
        out[:, j * hidden : (j + 1) * hidden] = value.astype(BF16)


def regroup(table, weight, *outs):
    width = outs[0].shape[2]
    for j in range(8):
        for d, out in enumerate(outs):

            @pl.when(table[j] >> 1 == d)
            def _(j=j, out=out):
                out[table[j] & 1] = weight[:, j * width : (j + 1) * width]


def gather_down(*refs):
    blocks, near, far = refs[:4], refs[4], refs[5]
    for d, block in enumerate(blocks):
        near[d] = block[0]
        far[d] = block[1]


def finish_input(residual, total, part, routes, out, sent):
    value = residual[...].astype(F32) + (total[...] + part[...].astype(F32))
    width = out.shape[1]
    out[...] = value.astype(BF16)
    sent[:, :width] = value.astype(BF16)
    sent[:, width:] = routes[...]


def contract(near, far, other_near, other_far, *refs):
    blocks, outs = refs[:8], refs[8:]
    total = None
    for i, block in enumerate(blocks):
        own, other = (far, other_far) if i & 1 else (near, other_near)
        term = dot(block[...], jnp.concatenate([own[i >> 1], other[i >> 1]], axis=0))
        total = term if total is None else total + term
    part = outs[0].shape[0]
    for d, out in enumerate(outs):
        out[...] = total[d * part : (d + 1) * part].astype(BF16)


def combine(table, choices, *refs):
    parts, outs, sums = refs[:4], refs[4:8], refs[8]
    total = None
    places = lax.broadcasted_iota(jnp.int32, (choices.shape[0], 2 * CAPACITY), 1).astype(F32)
    for d, block in enumerate(parts):
        weight = jnp.where(places == choices[:, d : d + 1], choices[:, 4 + d : 5 + d], 0.0)
        high = weight.astype(BF16)
        low = (weight - high.astype(F32)).astype(BF16)
        term = dot(high, block[...]) + dot(low, block[...])
        total = term if total is None else total + term
    sums[...] = total
    count, width = outs[0].shape
    for k, out in enumerate(outs):
        at = pl.ds(pl.multiple_of(table[k] * count, count), count)

        @pl.when(table[4 + k] == 0)
        def _(at=at, out=out):
            out[...] = sums[at, :width].astype(BF16)

        @pl.when(table[4 + k] == 1)
        def _(at=at, out=out):
            out[...] = sums[at, width:].astype(BF16)


def struct(*shape, dtype=BF16):
    return jax.ShapeDtypeStruct(shape, dtype)


def tie(value, *others):
    return lax.optimization_barrier((value, *others))[0]


def local(
    queries,
    latents,
    value_up,
    out_proj,
    residual,
    expert_gate,
    expert_up,
    expert_down,
    route_ids,
    route_gates,
):
    tokens, heads, feature_width = queries.shape
    keys = latents.shape[0]
    value_width = value_up.shape[2]
    scale = (value_width + feature_width - value_up.shape[1]) ** (-0.5)
    width = out_proj.shape[1]
    x, z, core = (lax.axis_index(axis) for axis in CTX)
    plane, row = (lax.axis_index(axis) for axis in EP)
    chips = [(((x - dx) & 3), (z ^ dz)) for dx, dz in PLANE]
    owners = [cx * 4 + cz * 2 + (core ^ dk) for dk in range(2) for cx, cz in chips]
    me = x * 4 + z * 2 + core

    first = keys * 16 - tokens * 16 + me * tokens
    b_k = [(plane & 1) ^ k0 for _, k0 in STEPS] + [(plane >> 1) ^ k1 for k1, _ in STEPS]
    entries = {
        "regroup": [(((j >> 1) - x) & 3) * 2 + (z ^ (j & 1)) for j in range(8)],
        "attend": owners + [first],
        "project": [cz * 4 + cx for cx, cz in chips]
        + [((row & 1) ^ k0 ^ core) * 2 + ((row >> 1) ^ k1) for k1, k0 in STEPS],
        "add_parts": [plane],
        "join": [core],
        "combine": b_k,
        "place": [(plane & 1) ^ k0 for k0 in (0, 1)] + [plane * 4 + ((row + d) & 3) for d in range(4)],
        "early": [chips[i][0] * 2 + chips[i][1] for i in EARLY],
        "late": [chips[i][0] * 2 + chips[i][1] for i in LATE],
    }
    starts, table = {}, []
    for name, values in entries.items():
        starts[name] = len(table)
        table += values
    table = jnp.stack(table).astype(jnp.int32)

    rows = jnp.transpose(queries, (1, 0, 2)).reshape(heads * tokens, feature_width)
    gathered = gather_wide(jnp.transpose(latents), [])
    hidden_width = expert_gate.shape[2]
    down = call(
        regroup,
        [struct(2, hidden_width, 2 * width)] * 4,
        start=starts["regroup"],
        name="regroup",
    )(table, expert_down[0])
    down = list(down)
    gathered[6], rows, down[0] = lax.optimization_barrier((gathered[6], rows, down[0]))
    swapped = [shift(block, "core", 1) for block in gathered]
    out_weight = jnp.transpose(out_proj)
    out_swapped = shift(tie(out_weight, *gathered), "core", 1)
    gates = []
    rest = route_gates
    for _ in range(3):
        gates.append(rest.astype(BF16))
        rest = rest - gates[-1].astype(F32)
    routes = jnp.concatenate([route_ids.astype(BF16), *gates], axis=1)

    gate = expert_gate.reshape(8, 2 * width, hidden_width)
    up = expert_up.reshape(8, 2 * width, hidden_width)
    gate_swapped = shift(tie(gate, *swapped), "core", 1)
    down[1] = shift(tie(down[1], *gathered), "x", 1)
    down[3] = shift(tie(down[3], *gathered), "x", 3)
    head_out = call(
        functools.partial(attend, scale, tokens),
        struct(tokens, heads * value_width),
        [pltpu.VMEM((heads * tokens, 16 * keys), F32)],
        vmem=20 << 20,
        flops=10 << 30,
        start=starts["attend"],
        name="attend",
    )(table, rows, value_up, *gathered, *swapped)

    head_out, out_swapped, down[1], down[3], gate_swapped = lax.optimization_barrier(
        (head_out, out_swapped, down[1], down[3], gate_swapped)
    )

    count = route_ids.shape[0]

    gathered_heads = gather_plane(head_out)
    parts = call(
        project,
        [struct(2 * tokens, 2 * width)] * 4,
        [
            pltpu.VMEM((8 * tokens, heads * value_width), BF16),
            pltpu.VMEM((16 * tokens, width), BF16),
        ],
        vmem=16 << 20,
        flops=2 << 30,
        start=starts["project"],
        name="project",
    )(
        table,
        out_weight,
        out_swapped,
        *gathered_heads,
    )
    down[2] = shift(tie(down[2], parts[0]), "x", 2)
    parts = [
        permute(part, ("core", "y"), lambda c, y: (y & 1, ((y >> 1) ^ k1) * 2 + (c ^ k0)))
        for part, (k1, k0) in zip(parts, STEPS)
    ]
    kept, sent = call(
        add_parts,
        [struct(2 * count, width, dtype=F32), struct(2 * count, width)],
        [pltpu.VMEM((4 * count, width), F32)],
        start=starts["add_parts"],
        name="add_parts",
    )(table, *parts)
    down[2], kept, sent = lax.optimization_barrier((down[2], kept, sent))
    up_swapped = shift(tie(up, kept), "core", 1)
    near, far = call(
        gather_down, [struct(4, hidden_width, 2 * width)] * 2, name="gather_down"
    )(*down)
    kept, sent = call(
        add_pair,
        [struct(count, width, dtype=F32), struct(count, width)],
        [pltpu.VMEM((2 * count, width), F32)],
        start=starts["add_parts"],
        name="add_pair",
    )(table, kept, shift(sent, "z_hi", 2))
    part = permute(sent, ("core", "z_hi"), lambda c, p: (c, p ^ 1))
    moe_input, routed_input = call(
        finish_input,
        [struct(count, width), struct(count, width + routes.shape[1])],
        name="finish_input",
    )(residual, kept, part, routes)
    routed_input, near, far, up_swapped = lax.optimization_barrier(
        (routed_input, near, far, up_swapped)
    )

    joined = call(
        join, struct(count, 2 * width + routes.shape[1]), start=starts["join"], name="join"
    )(table, routed_input, shift(routed_input, "core", 1))
    planes = [
        permute(joined, ("core", "z_hi"), lambda c, p: (p >> 1, 2 * c + (k0 ^ (p & 1))))
        for k0 in (0, 1)
    ]
    *outgoing, choices = call(
        place,
        [struct(2 * CAPACITY, 2 * width)] * 4 + [struct(2 * count, 8, dtype=F32)],
        [pltpu.VMEM((2 * count, 2 * width), BF16), pltpu.VMEM((2 * count, routes.shape[1]), F32)],
        start=starts["place"],
        name="place",
    )(table, *planes)
    arrived = [outgoing[0]] + [shift(outgoing[d], "y", d) for d in (1, 2, 3)]
    arrived = jnp.concatenate(arrived, axis=0)
    near, arrived = lax.optimization_barrier((near, arrived))
    slots = gather_wide(arrived, [])
    far = shift(tie(far, slots[1]), "z_lo", 1)
    near_swapped = shift(tie(near, slots[1]), "core", 1)

    weights = (gate, up, gate_swapped, up_swapped)
    part = struct(8 * CAPACITY, 4 * hidden_width, dtype=F32)
    hidden = ()
    last = struct(8 * CAPACITY, 2 * hidden_width)
    for name, some, out in (("early", EARLY, part), ("late", LATE, last)):
        hidden = call(
            functools.partial(expand, len(hidden)),
            out,
            vmem=16 << 20,
            flops=len(some) * (512 << 20),
            start=starts[name],
            name="expand",
        )(table, *hidden, *weights, *[slots[i] for i in some])
        hidden = (hidden,)
    (hidden,) = hidden
    hidden, near_swapped, far = lax.optimization_barrier((hidden, near_swapped, far))
    far_swapped = shift(far, "core", 1)
    hidden = gather_plane(hidden)
    results = call(
        contract,
        [struct(2 * CAPACITY, 2 * width)] * 4,
        vmem=16 << 20,
        flops=2 << 30,
        name="contract",
    )(near, far, near_swapped, far_swapped, *hidden)

    returned = [results[0]] + [shift(results[d], "y", -d) for d in (1, 2, 3)]
    sums = call(
        combine,
        [struct(count, width)] * 4,
        [pltpu.VMEM((2 * count, 2 * width), F32)],
        start=starts["combine"],
        name="combine",
    )(table, choices, *returned)
    routed = None
    for part, (k1, k0) in zip(sums, STEPS):
        part = permute(
            part,
            ("core", "z_hi"),
            lambda c, p: (p >> 1, ((c ^ k1) << 1) | ((p & 1) ^ k0)),
        ).astype(F32)
        routed = part if routed is None else routed + part
    return (moe_input.astype(F32) + routed).astype(BF16)


def solution(mesh):
    split = Mesh(mesh.devices.reshape(tuple(SIZES.values())), tuple(SIZES))
    return jax.shard_map(
        local,
        mesh=split,
        in_specs=(
            P(CTX, EP, None),
            P(CTX, None),
            P(EP, None, None),
            P(EP, CTX),
            P(EP, CTX),
            P(EP, None, CTX),
            P(EP, None, CTX),
            P(EP, CTX, None),
            P(EP, None),
            P(EP, None),
        ),
        out_specs=P(EP, CTX),
        check_vma=False,
    )
```

```python
import functools

import jax
import jax.numpy as jnp
from jax import lax
from jax.experimental import pallas as pl
from jax.experimental.pallas import tpu as pltpu
from jax.sharding import Mesh
from jax.sharding import PartitionSpec as P

NEG = -1e30
CTX = ("x", "z_lo", "core")
EP = ("z_hi", "y")
SIZES = {"x": 4, "z_lo": 2, "core": 2, "z_hi": 4, "y": 4}
CAPACITY = 36
F32, BF16 = jnp.float32, jnp.bfloat16
VMEM = pl.BlockSpec(memory_space=pltpu.VMEM)
SMEM = pl.BlockSpec(memory_space=pltpu.SMEM)


def shift(value, axis, by):
    size = SIZES[axis]
    return lax.ppermute(value, axis, [(i, (i + by) % size) for i in range(size)])


def permute(value, axes, source):
    first, second = (SIZES[axis] for axis in axes)
    pairs = []
    for i in range(first):
        for j in range(second):
            p, q = source(i, j)
            pairs.append((p * second + q, i * second + j))
    return lax.ppermute(value, axes, pairs)


def swap(value, axis, flip):
    return lax.ppermute(value, axis, [(i, i ^ flip) for i in range(SIZES[axis])])


def gather_plane(own):
    other = shift(own, "z_lo", 1)
    blocks = {}
    for dz, block in ((0, own), (1, other)):
        blocks[0, dz] = block
        for d in (1, 2, 3):
            blocks[d, dz] = swap(block, "x", d)
    return [blocks[key] for key in PLANE]


def gather_wide(own, together=None):
    first = shift(own, "z_lo", 1), shift(own, "x", 1), shift(own, "x", -1)
    if together is not None:
        first, together[:] = lax.optimization_barrier((first, together))
    other, before, after = first
    blocks = {(0, 0): own, (0, 1): other, (1, 0): before, (3, 0): after}
    blocks[1, 1] = shift(other, "x", 1)
    blocks[3, 1] = shift(other, "x", -1)
    blocks[2, 0] = shift(before, "x", 1)
    blocks[2, 1] = shift(blocks[3, 1], "x", -1)
    return [blocks[key] for key in PLANE]


PLANE = [(dx, dz) for dx in range(4) for dz in range(2)]
EARLY, LATE = [0, 1, 2, 6, 7], [3, 4, 5]
STEPS = [(0, 0), (0, 1), (1, 0), (1, 1)]
class Part:
    def __init__(self, table, start):
        self.table, self.start = table, start

    def __getitem__(self, index):
        return self.table[self.start + index]


def call(kernel, outs, scratch=(), vmem=8 << 20, flops=0, start=None, name=None):
    scalars = 0 if start is None else 1

    def body(*refs):
        if scalars:
            refs = (Part(refs[0], start), *refs[1:])
        kernel(*refs)

    def run(*args):
        return pl.pallas_call(
            body,
            out_shape=outs,
            in_specs=[SMEM] * scalars + [VMEM] * (len(args) - scalars),
            out_specs=jax.tree.map(lambda _: VMEM, outs),
            scratch_shapes=list(scratch),
            compiler_params=pltpu.CompilerParams(vmem_limit_bytes=vmem),
            cost_estimate=pl.CostEstimate(flops=flops, bytes_accessed=1 << 20, transcendentals=0),
            name=name,
        )(*args)

    return run


def dot(a, b, dims=((1,), (0,))):
    return lax.dot_general(a, b, (dims, ((), ())), preferred_element_type=F32)


def attend(scale, tokens, table, queries, value_up, *refs):
    blocks, out, scores = refs[:16], refs[16], refs[17]
    rows, _ = queries.shape
    keys = blocks[0].shape[1]
    heads, width, value_width = value_up.shape
    row_pos = table[16] + (lax.broadcasted_iota(jnp.int32, (rows, 1), 0) & (tokens - 1))
    lane = lax.broadcasted_iota(jnp.int32, (1, keys), 1)
    query = queries[...]
    top = jnp.full((rows, 128), NEG, F32)
    for i, block in enumerate(blocks):
        score = dot(query, block[...])
        score = jnp.where(table[i] * keys + lane <= row_pos, score, NEG)
        scores[:, i * keys : (i + 1) * keys] = score
        for j in range(0, keys, 128):
            top = jnp.maximum(top, score[:, j : j + 128])
    top = jnp.max(top, axis=1, keepdims=True)
    total = jnp.zeros((rows, 128), F32)
    added = jnp.zeros((rows, width), F32)
    for i, block in enumerate(blocks):
        raised = jnp.exp((scores[:, i * keys : (i + 1) * keys] - top) * scale)
        for j in range(0, keys, 128):
            total = total + raised[:, j : j + 128]
        added = added + dot(raised.astype(BF16), block[:width, :], ((1,), (1,)))
    context = (added / jnp.sum(total, axis=1, keepdims=True)).astype(BF16)
    for h in range(heads):
        head = dot(context[h * tokens : (h + 1) * tokens], value_up[h])
        out[:, h * value_width : (h + 1) * value_width] = head.astype(BF16)


def project(table, weight, swapped, *refs):
    blocks, outs, rows, sums = refs[:8], refs[8:12], refs[12], refs[13]
    count = blocks[0].shape[0]
    for i, block in enumerate(blocks):
        rows[pl.ds(pl.multiple_of(table[i] * count, count), count), :] = block[...]
    total = rows.shape[0]
    for which, columns in enumerate((weight, swapped)):
        sums[which * total : (which + 1) * total, :] = dot(
            rows[...], columns[...], ((1,), (1,))
        ).astype(BF16)
    quarter = total // 4
    width = outs[0].shape[1] // 2
    for k, out in enumerate(outs):
        for j in range(2):
            at = pl.multiple_of((2 * table[8 + k] + j) * quarter, quarter)
            out[:, j * width : (j + 1) * width] = sums[pl.ds(at, quarter), :]


def add_parts(table, *refs):
    parts, outs = refs[:4], refs[4:8]
    sums = refs[8]
    count, width = outs[0].shape
    total = parts[0][...].astype(F32)
    for part in parts[1:]:
        total = total + part[...].astype(F32)
    for j in range(2):
        sums[2 * j * count : 2 * (j + 1) * count, :] = total[:, j * width : (j + 1) * width]
    for d, out in enumerate(outs):
        at = pl.ds(pl.multiple_of((table[0] ^ d) * count, count), count)
        out[...] = sums[at, :].astype(out.dtype)


def join(table, own, other, out):
    width = (out.shape[1] - 32) // 2
    for core, (first, second) in enumerate(((own, other), (other, own))):

        @pl.when(table[0] == core)
        def _(first=first, second=second):
            out[:, :width] = first[:, :width]
            out[:, width : 2 * width] = second[:, :width]

    out[:, 2 * width :] = own[:, width:]


def place(table, *refs):
    blocks, outs, choices, rows, routes = refs[:2], refs[2:6], refs[6], refs[7], refs[8]
    count = blocks[0].shape[0]
    width = rows.shape[1]
    picks = (blocks[0].shape[1] - width) // 4
    for k, block in enumerate(blocks):
        at = pl.ds(pl.multiple_of(table[k] * count, count), count)
        rows[at, :] = block[:, :width]
        routes[at, :] = block[:, width:].astype(F32)

    total = rows.shape[0]
    index = lax.broadcasted_iota(jnp.int32, (total, total), 0)
    other = lax.broadcasted_iota(jnp.int32, (total, total), 1)
    earlier = (other < index) & (other // count == index // count)
    earlier = jnp.where(earlier, 1.0, 0.0).astype(BF16)
    ids = routes[:, :picks]
    gates = routes[:, picks : 2 * picks] + (
        routes[:, 2 * picks : 3 * picks] + routes[:, 3 * picks :]
    )
    half = lax.broadcasted_iota(jnp.int32, (total, 1), 0) // count
    places = lax.broadcasted_iota(jnp.int32, (total, 2 * CAPACITY), 1).astype(F32)
    lanes = lax.broadcasted_iota(jnp.int32, (total, 128), 1)
    matches = [ids == table[2 + d].astype(F32) for d in range(4)]
    hits = [
        jnp.max(jnp.where(match, 1.0, 0.0), axis=1, keepdims=True) for match in matches
    ]
    spread = jnp.zeros((total, 128), F32)
    for d, hit in enumerate(hits):
        spread = jnp.where(lanes == d, hit, spread)
    before = dot(earlier, spread.astype(BF16))
    for d, out in enumerate(outs):
        weight = jnp.sum(jnp.where(matches[d], gates, 0.0), axis=1, keepdims=True)
        slot = before[:, d : d + 1] + (half * CAPACITY).astype(F32)
        slot = jnp.where(hits[d] > 0.0, slot, -1.0)
        choices[:, d : d + 1] = slot
        choices[:, 4 + d : 5 + d] = weight
        placing = jnp.where(places == slot, 1.0, 0.0).astype(BF16)
        out[...] = dot(placing, rows[...], ((0,), (0,))).astype(BF16)


def expand(before, table, *refs):
    sums, refs = (refs[0], refs[1:]) if before else (None, refs)
    weights, blocks, out = refs[:4], refs[4:-1], refs[-1]
    hidden = weights[0].shape[2]
    total = sums[...] if before else None
    for i, block in enumerate(blocks):
        weight = jnp.concatenate([weight[table[i]] for weight in weights], axis=1)
        term = dot(block[...], weight)
        total = term if total is None else total + term
    if not before:
        out[...] = total
        return
    for j in range(2):
        gated = total[:, 2 * j * hidden : (2 * j + 1) * hidden]
        upward = total[:, (2 * j + 1) * hidden : (2 * j + 2) * hidden]
        value = gated / (1.0 + jnp.exp(-gated)) * upward
        out[:, j * hidden : (j + 1) * hidden] = value.astype(BF16)


def regroup(table, weight, *outs):
    width = outs[0].shape[2]
    for j in range(8):
        for d, out in enumerate(outs):

            @pl.when(table[j] >> 1 == d)
            def _(j=j, out=out):
                out[table[j] & 1] = weight[:, j * width : (j + 1) * width]


def gather_down(*refs):
    blocks, near, far = refs[:4], refs[4], refs[5]
    for d, block in enumerate(blocks):
        near[d] = block[0]
        far[d] = block[1]


def finish_input(residual, total, *refs):
    parts, routes, out, sent = refs[:3], refs[3], refs[4], refs[5]
    value = residual[...].astype(F32) + total[...]
    for part in parts:
        value = value + part[...].astype(F32)
    width = out.shape[1]
    out[...] = value.astype(BF16)
    sent[:, :width] = value.astype(BF16)
    sent[:, width:] = routes[...]


def contract(near, far, other_near, other_far, *refs):
    blocks, outs = refs[:8], refs[8:]
    total = None
    for i, block in enumerate(blocks):
        own, other = (far, other_far) if i & 1 else (near, other_near)
        term = dot(block[...], jnp.concatenate([own[i >> 1], other[i >> 1]], axis=0))
        total = term if total is None else total + term
    part = outs[0].shape[0]
    for d, out in enumerate(outs):
        out[...] = total[d * part : (d + 1) * part].astype(BF16)


def combine(table, choices, *refs):
    parts, outs, sums = refs[:4], refs[4:8], refs[8]
    total = None
    places = lax.broadcasted_iota(jnp.int32, (choices.shape[0], 2 * CAPACITY), 1).astype(F32)
    for d, block in enumerate(parts):
        weight = jnp.where(places == choices[:, d : d + 1], choices[:, 4 + d : 5 + d], 0.0)
        high = weight.astype(BF16)
        low = (weight - high.astype(F32)).astype(BF16)
        term = dot(high, block[...]) + dot(low, block[...])
        total = term if total is None else total + term
    sums[...] = total
    count, width = outs[0].shape
    for k, out in enumerate(outs):
        at = pl.ds(pl.multiple_of(table[k] * count, count), count)

        @pl.when(table[4 + k] == 0)
        def _(at=at, out=out):
            out[...] = sums[at, :width].astype(BF16)

        @pl.when(table[4 + k] == 1)
        def _(at=at, out=out):
            out[...] = sums[at, width:].astype(BF16)


def struct(*shape, dtype=BF16):
    return jax.ShapeDtypeStruct(shape, dtype)


def tie(value, *others):
    return lax.optimization_barrier((value, *others))[0]


def local(
    queries,
    latents,
    value_up,
    out_proj,
    residual,
    expert_gate,
    expert_up,
    expert_down,
    route_ids,
    route_gates,
):
    tokens, heads, feature_width = queries.shape
    keys = latents.shape[0]
    value_width = value_up.shape[2]
    scale = (value_width + feature_width - value_up.shape[1]) ** (-0.5)
    width = out_proj.shape[1]
    x, z, core = (lax.axis_index(axis) for axis in CTX)
    plane, row = (lax.axis_index(axis) for axis in EP)
    chips = [(((x - dx) & 3), (z ^ dz)) for dx, dz in PLANE]
    flips = [(x ^ dx, z ^ dz) for dx, dz in PLANE]
    owners = [cx * 4 + cz * 2 + (core ^ dk) for dk in range(2) for cx, cz in chips]
    me = x * 4 + z * 2 + core

    first = keys * 16 - tokens * 16 + me * tokens
    b_k = [(plane & 1) ^ k0 for _, k0 in STEPS] + [(plane >> 1) ^ k1 for k1, _ in STEPS]
    entries = {
        "regroup": [((j >> 1) ^ x) * 2 + (z ^ (j & 1)) for j in range(8)],
        "attend": owners + [first],
        "project": [cz * 4 + cx for cx, cz in flips]
        + [((row & 1) ^ k0 ^ core) * 2 + ((row >> 1) ^ k1) for k1, k0 in STEPS],
        "add_parts": [plane],
        "join": [core],
        "combine": b_k,
        "place": [(plane & 1) ^ k0 for k0 in (0, 1)] + [plane * 4 + (row ^ d) for d in range(4)],
        "early": [chips[i][0] * 2 + chips[i][1] for i in EARLY],
        "late": [chips[i][0] * 2 + chips[i][1] for i in LATE],
    }
    starts, table = {}, []
    for name, values in entries.items():
        starts[name] = len(table)
        table += values
    table = jnp.stack(table).astype(jnp.int32)

    rows = jnp.transpose(queries, (1, 0, 2)).reshape(heads * tokens, feature_width)
    gathered = gather_wide(jnp.transpose(latents), [])
    hidden_width = expert_gate.shape[2]
    down = call(
        regroup,
        [struct(2, hidden_width, 2 * width)] * 4,
        start=starts["regroup"],
        name="regroup",
    )(table, expert_down[0])
    down = list(down)
    gathered[6], rows, down[0] = lax.optimization_barrier((gathered[6], rows, down[0]))
    swapped = [shift(block, "core", 1) for block in gathered]
    out_weight = jnp.transpose(out_proj)
    out_swapped = shift(tie(out_weight, *gathered), "core", 1)
    gates = []
    rest = route_gates
    for _ in range(3):
        gates.append(rest.astype(BF16))
        rest = rest - gates[-1].astype(F32)
    routes = jnp.concatenate([route_ids.astype(BF16), *gates], axis=1)

    down[1] = swap(tie(down[1], *gathered), "x", 1)
    down[3] = swap(tie(down[3], *gathered), "x", 3)
    head_out = call(
        functools.partial(attend, scale, tokens),
        struct(tokens, heads * value_width),
        [pltpu.VMEM((heads * tokens, 16 * keys), F32)],
        vmem=20 << 20,
        flops=10 << 30,
        start=starts["attend"],
        name="attend",
    )(table, rows, value_up, *gathered, *swapped)

    head_out, out_swapped, down[1], down[3] = lax.optimization_barrier(
        (head_out, out_swapped, down[1], down[3])
    )

    count = route_ids.shape[0]

    gathered_heads = gather_plane(head_out)
    parts = call(
        project,
        [struct(2 * tokens, 2 * width)] * 4,
        [
            pltpu.VMEM((8 * tokens, heads * value_width), BF16),
            pltpu.VMEM((16 * tokens, width), BF16),
        ],
        vmem=16 << 20,
        flops=2 << 30,
        start=starts["project"],
        name="project",
    )(
        table,
        out_weight,
        out_swapped,
        *gathered_heads,
    )
    down[2] = swap(tie(down[2], parts[0]), "x", 2)
    parts = [
        permute(part, ("core", "y"), lambda c, y: (y & 1, ((y >> 1) ^ k1) * 2 + (c ^ k0)))
        for part, (k1, k0) in zip(parts, STEPS)
    ]
    sums = call(
        add_parts,
        [struct(count, width, dtype=F32)] + [struct(count, width)] * 3,
        [pltpu.VMEM((4 * count, width), F32)],
        start=starts["add_parts"],
        name="add_parts",
    )(table, *parts)
    down[2], *sums = lax.optimization_barrier((down[2], *sums))
    near, far = call(
        gather_down, [struct(4, hidden_width, 2 * width)] * 2, name="gather_down"
    )(*down)
    moe_input, routed_input = call(
        finish_input,
        [struct(count, width), struct(count, width + routes.shape[1])],
        name="finish_input",
    )(residual, sums[0], *[swap(sums[d], "z_hi", d) for d in (1, 2, 3)], routes)
    routed_input, near, far = lax.optimization_barrier((routed_input, near, far))

    joined = call(
        join, struct(count, 2 * width + routes.shape[1]), start=starts["join"], name="join"
    )(table, routed_input, shift(routed_input, "core", 1))
    planes = [
        permute(joined, ("core", "z_hi"), lambda c, p: (p >> 1, 2 * c + (k0 ^ (p & 1))))
        for k0 in (0, 1)
    ]
    *outgoing, choices = call(
        place,
        [struct(2 * CAPACITY, 2 * width)] * 4 + [struct(2 * count, 8, dtype=F32)],
        [pltpu.VMEM((2 * count, 2 * width), BF16), pltpu.VMEM((2 * count, routes.shape[1]), F32)],
        start=starts["place"],
        name="place",
    )(table, *planes)
    arrived = [outgoing[0]] + [swap(outgoing[d], "y", d) for d in (1, 2, 3)]
    arrived = jnp.concatenate(arrived, axis=0)
    gate, up, near = lax.optimization_barrier((expert_gate, expert_up, near, arrived))[:3]
    gate = gate.reshape(8, 2 * width, hidden_width)
    up = up.reshape(8, 2 * width, hidden_width)
    swapped = [shift(gate, "core", 1), shift(up, "core", 1)]
    slots = gather_wide(arrived, swapped)
    gate_swapped, up_swapped = swapped
    far = shift(tie(far, slots[1]), "z_lo", 1)
    near_swapped = shift(tie(near, slots[1]), "core", 1)

    weights = (gate, up, gate_swapped, up_swapped)
    part = struct(8 * CAPACITY, 4 * hidden_width, dtype=F32)
    hidden = ()
    last = struct(8 * CAPACITY, 2 * hidden_width)
    for name, some, out in (("early", EARLY, part), ("late", LATE, last)):
        hidden = call(
            functools.partial(expand, len(hidden)),
            out,
            vmem=16 << 20,
            flops=len(some) * (512 << 20),
            start=starts[name],
            name="expand",
        )(table, *hidden, *weights, *[slots[i] for i in some])
        hidden = (hidden,)
    (hidden,) = hidden
    hidden, near_swapped, far = lax.optimization_barrier((hidden, near_swapped, far))
    far_swapped = shift(far, "core", 1)
    hidden = gather_plane(hidden)
    results = call(
        contract,
        [struct(2 * CAPACITY, 2 * width)] * 4,
        vmem=16 << 20,
        flops=2 << 30,
        name="contract",
    )(near, far, near_swapped, far_swapped, *hidden)

    returned = [results[0]] + [swap(results[d], "y", d) for d in (1, 2, 3)]
    sums = call(
        combine,
        [struct(count, width)] * 4,
        [pltpu.VMEM((2 * count, 2 * width), F32)],
        start=starts["combine"],
        name="combine",
    )(table, choices, *returned)
    routed = None
    for part, (k1, k0) in zip(sums, STEPS):
        part = permute(
            part,
            ("core", "z_hi"),
            lambda c, p: (p >> 1, ((c ^ k1) << 1) | ((p & 1) ^ k0)),
        ).astype(F32)
        routed = part if routed is None else routed + part
    return (moe_input.astype(F32) + routed).astype(BF16)


def solution(mesh):
    split = Mesh(mesh.devices.reshape(tuple(SIZES.values())), tuple(SIZES))
    return jax.shard_map(
        local,
        mesh=split,
        in_specs=(
            P(CTX, EP, None),
            P(CTX, None),
            P(EP, None, None),
            P(EP, CTX),
            P(EP, CTX),
            P(EP, None, CTX),
            P(EP, None, CTX),
            P(EP, CTX, None),
            P(EP, None),
            P(EP, None),
        ),
        out_specs=P(EP, CTX),
        check_vma=False,
    )
```

```python
import functools

import jax
import jax.numpy as jnp
from jax import lax
from jax.experimental import pallas as pl
from jax.experimental.pallas import tpu as pltpu
from jax.sharding import Mesh
from jax.sharding import PartitionSpec as P

NEG = -1e30
CTX = ("x", "z_lo", "core")
EP = ("z_hi", "y")
SIZES = {"x": 4, "z_lo": 2, "core": 2, "z_hi": 4, "y": 4}
CAPACITY = 36
F32, BF16 = jnp.float32, jnp.bfloat16
VMEM = pl.BlockSpec(memory_space=pltpu.VMEM)
SMEM = pl.BlockSpec(memory_space=pltpu.SMEM)


def shift(value, axis, by):
    size = SIZES[axis]
    return lax.ppermute(value, axis, [(i, (i + by) % size) for i in range(size)])


def permute(value, axes, source):
    first, second = (SIZES[axis] for axis in axes)
    pairs = []
    for i in range(first):
        for j in range(second):
            p, q = source(i, j)
            pairs.append((p * second + q, i * second + j))
    return lax.ppermute(value, axes, pairs)


def swap(value, axis, flip):
    return lax.ppermute(value, axis, [(i, i ^ flip) for i in range(SIZES[axis])])


def gather_plane(own):
    other = shift(own, "z_lo", 1)
    blocks = {}
    for dz, block in ((0, own), (1, other)):
        blocks[0, dz] = block
        for d in (1, 2, 3):
            blocks[d, dz] = swap(block, "x", d)
    return [blocks[key] for key in PLANE]


def gather_wide(own, together=None):
    first = shift(own, "z_lo", 1), shift(own, "x", 1), shift(own, "x", -1)
    if together is not None:
        first, together[:] = lax.optimization_barrier((first, together))
    other, before, after = first
    blocks = {(0, 0): own, (0, 1): other, (1, 0): before, (3, 0): after}
    blocks[1, 1] = shift(other, "x", 1)
    blocks[3, 1] = shift(other, "x", -1)
    blocks[2, 0] = shift(before, "x", 1)
    blocks[2, 1] = shift(blocks[3, 1], "x", -1)
    return [blocks[key] for key in PLANE]


PLANE = [(dx, dz) for dx in range(4) for dz in range(2)]
EARLY, LATE = [0, 1, 2, 6, 7], [3, 4, 5]
STEPS = [(0, 0), (0, 1), (1, 0), (1, 1)]
class Part:
    def __init__(self, table, start):
        self.table, self.start = table, start

    def __getitem__(self, index):
        return self.table[self.start + index]


def call(kernel, outs, scratch=(), vmem=4 << 20, flops=0, start=None, name=None):
    scalars = 0 if start is None else 1

    def body(*refs):
        if scalars:
            refs = (Part(refs[0], start), *refs[1:])
        kernel(*refs)

    def run(*args):
        return pl.pallas_call(
            body,
            out_shape=outs,
            in_specs=[SMEM] * scalars + [VMEM] * (len(args) - scalars),
            out_specs=jax.tree.map(lambda _: VMEM, outs),
            scratch_shapes=list(scratch),
            compiler_params=pltpu.CompilerParams(vmem_limit_bytes=vmem),
            cost_estimate=pl.CostEstimate(flops=flops, bytes_accessed=1 << 20, transcendentals=0),
            name=name,
        )(*args)

    return run


def dot(a, b, dims=((1,), (0,))):
    return lax.dot_general(a, b, (dims, ((), ())), preferred_element_type=F32)


def attend(scale, tokens, table, queries, value_up, *refs):
    blocks, out, scores = refs[:16], refs[16], refs[17]
    rows, _ = queries.shape
    keys = blocks[0].shape[1]
    heads, width, value_width = value_up.shape
    row_pos = table[16] + (lax.broadcasted_iota(jnp.int32, (rows, 1), 0) & (tokens - 1))
    lane = lax.broadcasted_iota(jnp.int32, (1, keys), 1)
    query = queries[...]
    top = jnp.full((rows, 128), NEG, F32)
    for i, block in enumerate(blocks):
        score = dot(query, block[...])
        score = jnp.where(table[i] * keys + lane <= row_pos, score, NEG)
        scores[:, i * keys : (i + 1) * keys] = score
        for j in range(0, keys, 128):
            top = jnp.maximum(top, score[:, j : j + 128])
    top = jnp.max(top, axis=1, keepdims=True)
    total = jnp.zeros((rows, 128), F32)
    added = jnp.zeros((rows, width), F32)
    for i, block in enumerate(blocks):
        raised = jnp.exp((scores[:, i * keys : (i + 1) * keys] - top) * scale)
        for j in range(0, keys, 128):
            total = total + raised[:, j : j + 128]
        added = added + dot(raised.astype(BF16), block[:width, :], ((1,), (1,)))
    context = (added / jnp.sum(total, axis=1, keepdims=True)).astype(BF16)
    for h in range(heads):
        head = dot(context[h * tokens : (h + 1) * tokens], value_up[h])
        out[:, h * value_width : (h + 1) * value_width] = head.astype(BF16)


def project(table, weight, swapped, *refs):
    blocks, outs, rows, sums = refs[:8], refs[8:12], refs[12], refs[13]
    count = blocks[0].shape[0]
    for i, block in enumerate(blocks):
        rows[pl.ds(pl.multiple_of(table[i] * count, count), count), :] = block[...]
    total = rows.shape[0]
    for which, columns in enumerate((weight, swapped)):
        sums[which * total : (which + 1) * total, :] = dot(
            rows[...], columns[...], ((1,), (1,))
        ).astype(BF16)
    quarter = total // 4
    width = outs[0].shape[1] // 2
    for k, out in enumerate(outs):
        for j in range(2):
            at = pl.multiple_of((2 * table[8 + k] + j) * quarter, quarter)
            out[:, j * width : (j + 1) * width] = sums[pl.ds(at, quarter), :]


def add_parts(table, *refs):
    parts, outs = refs[:4], refs[4:8]
    sums = refs[8]
    count, width = outs[0].shape
    total = parts[0][...].astype(F32)
    for part in parts[1:]:
        total = total + part[...].astype(F32)
    for j in range(2):
        sums[2 * j * count : 2 * (j + 1) * count, :] = total[:, j * width : (j + 1) * width]
    for d, out in enumerate(outs):
        at = pl.ds(pl.multiple_of((table[0] ^ d) * count, count), count)
        out[...] = sums[at, :].astype(out.dtype)


def join(table, own, other, out):
    width = (out.shape[1] - 32) // 2
    for core, (first, second) in enumerate(((own, other), (other, own))):

        @pl.when(table[0] == core)
        def _(first=first, second=second):
            out[:, :width] = first[:, :width]
            out[:, width : 2 * width] = second[:, :width]

    out[:, 2 * width :] = own[:, width:]


def place(table, *refs):
    blocks, outs, choices, rows, routes = refs[:2], refs[2:6], refs[6], refs[7], refs[8]
    count = blocks[0].shape[0]
    width = rows.shape[1]
    picks = (blocks[0].shape[1] - width) // 4
    for k, block in enumerate(blocks):
        at = pl.ds(pl.multiple_of(table[k] * count, count), count)
        rows[at, :] = block[:, :width]
        routes[at, :] = block[:, width:].astype(F32)

    total = rows.shape[0]
    index = lax.broadcasted_iota(jnp.int32, (total, total), 0)
    other = lax.broadcasted_iota(jnp.int32, (total, total), 1)
    earlier = (other < index) & (other // count == index // count)
    earlier = jnp.where(earlier, 1.0, 0.0).astype(BF16)
    ids = routes[:, :picks]
    gates = routes[:, picks : 2 * picks] + (
        routes[:, 2 * picks : 3 * picks] + routes[:, 3 * picks :]
    )
    half = lax.broadcasted_iota(jnp.int32, (total, 1), 0) // count
    places = lax.broadcasted_iota(jnp.int32, (total, 2 * CAPACITY), 1).astype(F32)
    lanes = lax.broadcasted_iota(jnp.int32, (total, 128), 1)
    matches = [ids == table[2 + d].astype(F32) for d in range(4)]
    hits = [
        jnp.max(jnp.where(match, 1.0, 0.0), axis=1, keepdims=True) for match in matches
    ]
    spread = jnp.zeros((total, 128), F32)
    for d, hit in enumerate(hits):
        spread = jnp.where(lanes == d, hit, spread)
    before = dot(earlier, spread.astype(BF16))
    for d, out in enumerate(outs):
        weight = jnp.sum(jnp.where(matches[d], gates, 0.0), axis=1, keepdims=True)
        slot = before[:, d : d + 1] + (half * CAPACITY).astype(F32)
        slot = jnp.where(hits[d] > 0.0, slot, -1.0)
        choices[:, d : d + 1] = slot
        choices[:, 4 + d : 5 + d] = weight
        placing = jnp.where(places == slot, 1.0, 0.0).astype(BF16)
        out[...] = dot(placing, rows[...], ((0,), (0,))).astype(BF16)


def expand(before, table, *refs):
    sums, refs = (refs[0], refs[1:]) if before else (None, refs)
    weights, blocks, out = refs[:4], refs[4:-1], refs[-1]
    hidden = weights[0].shape[2]
    total = sums[...] if before else None
    for i, block in enumerate(blocks):
        weight = jnp.concatenate([weight[table[i]] for weight in weights], axis=1)
        term = dot(block[...], weight)
        total = term if total is None else total + term
    if not before:
        out[...] = total
        return
    for j in range(2):
        gated = total[:, 2 * j * hidden : (2 * j + 1) * hidden]
        upward = total[:, (2 * j + 1) * hidden : (2 * j + 2) * hidden]
        value = gated / (1.0 + jnp.exp(-gated)) * upward
        out[:, j * hidden : (j + 1) * hidden] = value.astype(BF16)


def regroup(table, weight, *outs):
    width = outs[0].shape[2]
    for j in range(8):
        for d, out in enumerate(outs):

            @pl.when(table[j] >> 1 == d)
            def _(j=j, out=out):
                out[table[j] & 1] = weight[:, j * width : (j + 1) * width]


def gather_down(*refs):
    blocks, near, far = refs[:4], refs[4], refs[5]
    for d, block in enumerate(blocks):
        near[d] = block[0]
        far[d] = block[1]


def finish_input(residual, total, *refs):
    parts, routes, out, sent = refs[:3], refs[3], refs[4], refs[5]
    value = residual[...].astype(F32) + total[...]
    for part in parts:
        value = value + part[...].astype(F32)
    width = out.shape[1]
    out[...] = value.astype(BF16)
    sent[:, :width] = value.astype(BF16)
    sent[:, width:] = routes[...]


def contract(near, far, other_near, other_far, *refs):
    blocks, outs = refs[:8], refs[8:]
    total = None
    for i, block in enumerate(blocks):
        own, other = (far, other_far) if i & 1 else (near, other_near)
        term = dot(block[...], jnp.concatenate([own[i >> 1], other[i >> 1]], axis=0))
        total = term if total is None else total + term
    part = outs[0].shape[0]
    for d, out in enumerate(outs):
        out[...] = total[d * part : (d + 1) * part].astype(BF16)


def combine(table, choices, *refs):
    parts, outs, sums = refs[:4], refs[4:8], refs[8]
    total = None
    places = lax.broadcasted_iota(jnp.int32, (choices.shape[0], 2 * CAPACITY), 1).astype(F32)
    for d, block in enumerate(parts):
        weight = jnp.where(places == choices[:, d : d + 1], choices[:, 4 + d : 5 + d], 0.0)
        high = weight.astype(BF16)
        low = (weight - high.astype(F32)).astype(BF16)
        term = dot(high, block[...]) + dot(low, block[...])
        total = term if total is None else total + term
    sums[...] = total
    count, width = outs[0].shape
    for k, out in enumerate(outs):
        at = pl.ds(pl.multiple_of(table[k] * count, count), count)

        @pl.when(table[4 + k] == 0)
        def _(at=at, out=out):
            out[...] = sums[at, :width].astype(BF16)

        @pl.when(table[4 + k] == 1)
        def _(at=at, out=out):
            out[...] = sums[at, width:].astype(BF16)


def struct(*shape, dtype=BF16):
    return jax.ShapeDtypeStruct(shape, dtype)


def tie(value, *others):
    return lax.optimization_barrier((value, *others))[0]


def local(
    queries,
    latents,
    value_up,
    out_proj,
    residual,
    expert_gate,
    expert_up,
    expert_down,
    route_ids,
    route_gates,
):
    tokens, heads, feature_width = queries.shape
    keys = latents.shape[0]
    value_width = value_up.shape[2]
    scale = (value_width + feature_width - value_up.shape[1]) ** (-0.5)
    width = out_proj.shape[1]
    x, z, core = (lax.axis_index(axis) for axis in CTX)
    plane, row = (lax.axis_index(axis) for axis in EP)
    chips = [(((x - dx) & 3), (z ^ dz)) for dx, dz in PLANE]
    flips = [(x ^ dx, z ^ dz) for dx, dz in PLANE]
    owners = [cx * 4 + cz * 2 + (core ^ dk) for dk in range(2) for cx, cz in chips]
    me = x * 4 + z * 2 + core

    first = keys * 16 - tokens * 16 + me * tokens
    b_k = [(plane & 1) ^ k0 for _, k0 in STEPS] + [(plane >> 1) ^ k1 for k1, _ in STEPS]
    entries = {
        "regroup": [((j >> 1) ^ x) * 2 + (z ^ (j & 1)) for j in range(8)],
        "attend": owners + [first],
        "project": [cz * 4 + cx for cx, cz in flips]
        + [((row & 1) ^ k0 ^ core) * 2 + ((row >> 1) ^ k1) for k1, k0 in STEPS],
        "add_parts": [plane],
        "join": [core],
        "combine": b_k,
        "place": [(plane & 1) ^ k0 for k0 in (0, 1)] + [plane * 4 + (row ^ d) for d in range(4)],
        "early": [chips[i][0] * 2 + chips[i][1] for i in EARLY],
        "late": [chips[i][0] * 2 + chips[i][1] for i in LATE],
    }
    starts, table = {}, []
    for name, values in entries.items():
        starts[name] = len(table)
        table += values
    table = jnp.stack(table).astype(jnp.int32)

    rows = jnp.transpose(queries, (1, 0, 2)).reshape(heads * tokens, feature_width)
    gathered = gather_wide(jnp.transpose(latents), [])
    hidden_width = expert_gate.shape[2]
    down = call(
        regroup,
        [struct(2, hidden_width, 2 * width)] * 4,
        start=starts["regroup"],
        name="regroup",
    )(table, expert_down[0])
    down = list(down)
    gathered[6], rows, down[0] = lax.optimization_barrier((gathered[6], rows, down[0]))
    swapped = [shift(block, "core", 1) for block in gathered]
    out_weight = jnp.transpose(out_proj)
    out_swapped = shift(tie(out_weight, *gathered), "core", 1)
    gates = []
    rest = route_gates
    for _ in range(3):
        gates.append(rest.astype(BF16))
        rest = rest - gates[-1].astype(F32)
    routes = jnp.concatenate([route_ids.astype(BF16), *gates], axis=1)

    down[1] = swap(tie(down[1], *gathered), "x", 1)
    down[3] = swap(tie(down[3], *gathered), "x", 3)
    head_out = call(
        functools.partial(attend, scale, tokens),
        struct(tokens, heads * value_width),
        [pltpu.VMEM((heads * tokens, 16 * keys), F32)],
        vmem=13 << 20,
        flops=10 << 30,
        start=starts["attend"],
        name="attend",
    )(table, rows, value_up, *gathered, *swapped)

    head_out, out_swapped, down[1], down[3] = lax.optimization_barrier(
        (head_out, out_swapped, down[1], down[3])
    )

    count = route_ids.shape[0]

    gathered_heads = gather_plane(head_out)
    parts = call(
        project,
        [struct(2 * tokens, 2 * width)] * 4,
        [
            pltpu.VMEM((8 * tokens, heads * value_width), BF16),
            pltpu.VMEM((16 * tokens, width), BF16),
        ],
        vmem=6 << 20,
        flops=2 << 30,
        start=starts["project"],
        name="project",
    )(
        table,
        out_weight,
        out_swapped,
        *gathered_heads,
    )
    down[2] = swap(tie(down[2], parts[0]), "x", 2)
    parts = [
        permute(part, ("core", "y"), lambda c, y: (y & 1, ((y >> 1) ^ k1) * 2 + (c ^ k0)))
        for part, (k1, k0) in zip(parts, STEPS)
    ]
    sums = call(
        add_parts,
        [struct(count, width, dtype=F32)] + [struct(count, width)] * 3,
        [pltpu.VMEM((4 * count, width), F32)],
        start=starts["add_parts"],
        name="add_parts",
    )(table, *parts)
    down[2], *sums = lax.optimization_barrier((down[2], *sums))
    near, far = call(
        gather_down, [struct(4, hidden_width, 2 * width)] * 2, name="gather_down"
    )(*down)
    moe_input, routed_input = call(
        finish_input,
        [struct(count, width), struct(count, width + routes.shape[1])],
        name="finish_input",
    )(residual, sums[0], *[swap(sums[d], "z_hi", d) for d in (1, 2, 3)], routes)
    routed_input, near, far = lax.optimization_barrier((routed_input, near, far))

    joined = call(
        join, struct(count, 2 * width + routes.shape[1]), start=starts["join"], name="join"
    )(table, routed_input, shift(routed_input, "core", 1))
    planes = [
        permute(joined, ("core", "z_hi"), lambda c, p: (p >> 1, 2 * c + (k0 ^ (p & 1))))
        for k0 in (0, 1)
    ]
    *outgoing, choices = call(
        place,
        [struct(2 * CAPACITY, 2 * width)] * 4 + [struct(2 * count, 8, dtype=F32)],
        [pltpu.VMEM((2 * count, 2 * width), BF16), pltpu.VMEM((2 * count, routes.shape[1]), F32)],
        start=starts["place"],
        name="place",
    )(table, *planes)
    arrived = [outgoing[0]] + [swap(outgoing[d], "y", d) for d in (1, 2, 3)]
    arrived = jnp.concatenate(arrived, axis=0)
    gate, up, near = lax.optimization_barrier((expert_gate, expert_up, near, arrived))[:3]
    gate = gate.reshape(8, 2 * width, hidden_width)
    up = up.reshape(8, 2 * width, hidden_width)
    swapped = [shift(gate, "core", 1), shift(up, "core", 1)]
    slots = gather_wide(arrived, swapped)
    gate_swapped, up_swapped = swapped
    far = shift(tie(far, slots[1]), "z_lo", 1)
    near_swapped = shift(tie(near, slots[1]), "core", 1)

    weights = (gate, up, gate_swapped, up_swapped)
    part = struct(8 * CAPACITY, 4 * hidden_width, dtype=F32)
    hidden = ()
    last = struct(8 * CAPACITY, 2 * hidden_width)
    for name, some, out in (("early", EARLY, part), ("late", LATE, last)):
        hidden = call(
            functools.partial(expand, len(hidden)),
            out,
            vmem=6 << 20,
            flops=len(some) * (512 << 20),
            start=starts[name],
            name="expand",
        )(table, *hidden, *weights, *[slots[i] for i in some])
        hidden = (hidden,)
    (hidden,) = hidden
    hidden, near_swapped, far = lax.optimization_barrier((hidden, near_swapped, far))
    far_swapped = shift(far, "core", 1)
    hidden = gather_plane(hidden)
    results = call(
        contract,
        [struct(2 * CAPACITY, 2 * width)] * 4,
        vmem=6 << 20,
        flops=2 << 30,
        name="contract",
    )(near, far, near_swapped, far_swapped, *hidden)

    returned = [results[0]] + [swap(results[d], "y", d) for d in (1, 2, 3)]
    sums = call(
        combine,
        [struct(count, width)] * 4,
        [pltpu.VMEM((2 * count, 2 * width), F32)],
        start=starts["combine"],
        name="combine",
    )(table, choices, *returned)
    routed = None
    for part, (k1, k0) in zip(sums, STEPS):
        part = permute(
            part,
            ("core", "z_hi"),
            lambda c, p: (p >> 1, ((c ^ k1) << 1) | ((p & 1) ^ k0)),
        ).astype(F32)
        routed = part if routed is None else routed + part
    return (moe_input.astype(F32) + routed).astype(BF16)


def solution(mesh):
    split = Mesh(mesh.devices.reshape(tuple(SIZES.values())), tuple(SIZES))
    return jax.shard_map(
        local,
        mesh=split,
        in_specs=(
            P(CTX, EP, None),
            P(CTX, None),
            P(EP, None, None),
            P(EP, CTX),
            P(EP, CTX),
            P(EP, None, CTX),
            P(EP, None, CTX),
            P(EP, CTX, None),
            P(EP, None),
            P(EP, None),
        ),
        out_specs=P(EP, CTX),
        check_vma=False,
    )
```

```python
import functools

import jax
import jax.numpy as jnp
from jax import lax
from jax.experimental import pallas as pl
from jax.experimental.pallas import tpu as pltpu
from jax.sharding import Mesh
from jax.sharding import PartitionSpec as P

NEG = -1e30
CTX = ("x", "z_lo", "core")
EP = ("z_hi", "y")
SIZES = {"x": 4, "z_lo": 2, "core": 2, "z_hi": 4, "y": 4}
CAPACITY = 36
F32, BF16 = jnp.float32, jnp.bfloat16
VMEM = pl.BlockSpec(memory_space=pltpu.VMEM)
SMEM = pl.BlockSpec(memory_space=pltpu.SMEM)


def shift(value, axis, by):
    size = SIZES[axis]
    return lax.ppermute(value, axis, [(i, (i + by) % size) for i in range(size)])


def permute(value, axes, source):
    first, second = (SIZES[axis] for axis in axes)
    pairs = []
    for i in range(first):
        for j in range(second):
            p, q = source(i, j)
            pairs.append((p * second + q, i * second + j))
    return lax.ppermute(value, axes, pairs)


def gather_plane(own):
    other = shift(own, "z_lo", 1)
    blocks = {}
    for dz, block in ((0, own), (1, other)):
        blocks[0, dz] = block
        for d in (1, 2, 3):
            blocks[d, dz] = shift(block, "x", d)
    return [blocks[key] for key in PLANE]


def gather_wide(own, together=None):
    first = shift(own, "z_lo", 1), shift(own, "x", 1), shift(own, "x", -1)
    if together is not None:
        first, together[:] = lax.optimization_barrier((first, together))
    other, before, after = first
    blocks = {(0, 0): own, (0, 1): other, (1, 0): before, (3, 0): after}
    blocks[1, 1] = shift(other, "x", 1)
    blocks[3, 1] = shift(other, "x", -1)
    blocks[2, 0] = shift(before, "x", 1)
    blocks[2, 1] = shift(blocks[3, 1], "x", -1)
    return [blocks[key] for key in PLANE]


PLANE = [(dx, dz) for dx in range(4) for dz in range(2)]
EARLY, LATE = [0, 1, 2, 6, 7], [3, 4, 5]
STEPS = [(0, 0), (0, 1), (1, 0), (1, 1)]
class Part:
    def __init__(self, table, start):
        self.table, self.start = table, start

    def __getitem__(self, index):
        return self.table[self.start + index]


def call(kernel, outs, scratch=(), vmem=8 << 20, flops=0, start=None, name=None):
    scalars = 0 if start is None else 1

    def body(*refs):
        if scalars:
            refs = (Part(refs[0], start), *refs[1:])
        kernel(*refs)

    def run(*args):
        return pl.pallas_call(
            body,
            out_shape=outs,
            in_specs=[SMEM] * scalars + [VMEM] * (len(args) - scalars),
            out_specs=jax.tree.map(lambda _: VMEM, outs),
            scratch_shapes=list(scratch),
            compiler_params=pltpu.CompilerParams(vmem_limit_bytes=vmem),
            cost_estimate=pl.CostEstimate(flops=flops, bytes_accessed=1 << 20, transcendentals=0),
            name=name,
        )(*args)

    return run


def dot(a, b, dims=((1,), (0,))):
    return lax.dot_general(a, b, (dims, ((), ())), preferred_element_type=F32)


def attend(scale, tokens, table, queries, value_up, *refs):
    blocks, out, scores = refs[:16], refs[16], refs[17]
    rows, _ = queries.shape
    keys = blocks[0].shape[1]
    heads, width, value_width = value_up.shape
    row_pos = table[16] + (lax.broadcasted_iota(jnp.int32, (rows, 1), 0) & (tokens - 1))
    lane = lax.broadcasted_iota(jnp.int32, (1, keys), 1)
    query = queries[...]
    top = jnp.full((rows, 128), NEG, F32)
    for i, block in enumerate(blocks):
        score = dot(query, block[...])
        score = jnp.where(table[i] * keys + lane <= row_pos, score, NEG)
        scores[:, i * keys : (i + 1) * keys] = score
        for j in range(0, keys, 128):
            top = jnp.maximum(top, score[:, j : j + 128])
    top = jnp.max(top, axis=1, keepdims=True)
    total = jnp.zeros((rows, 128), F32)
    added = jnp.zeros((rows, width), F32)
    for i, block in enumerate(blocks):
        raised = jnp.exp((scores[:, i * keys : (i + 1) * keys] - top) * scale)
        for j in range(0, keys, 128):
            total = total + raised[:, j : j + 128]
        added = added + dot(raised.astype(BF16), block[:width, :], ((1,), (1,)))
    context = (added / jnp.sum(total, axis=1, keepdims=True)).astype(BF16)
    for h in range(heads):
        head = dot(context[h * tokens : (h + 1) * tokens], value_up[h])
        out[:, h * value_width : (h + 1) * value_width] = head.astype(BF16)


def project(table, weight, swapped, *refs):
    blocks, outs, rows, sums = refs[:8], refs[8:12], refs[12], refs[13]
    count = blocks[0].shape[0]
    for i, block in enumerate(blocks):
        rows[pl.ds(pl.multiple_of(table[i] * count, count), count), :] = block[...]
    total = rows.shape[0]
    for which, columns in enumerate((weight, swapped)):
        sums[which * total : (which + 1) * total, :] = dot(
            rows[...], columns[...], ((1,), (1,))
        ).astype(BF16)
    quarter = total // 4
    width = outs[0].shape[1] // 2
    for k, out in enumerate(outs):
        for j in range(2):
            at = pl.multiple_of((2 * table[8 + k] + j) * quarter, quarter)
            out[:, j * width : (j + 1) * width] = sums[pl.ds(at, quarter), :]


def add_parts(table, *refs):
    parts, outs = refs[:4], refs[4:8]
    sums = refs[8]
    count, width = outs[0].shape
    total = parts[0][...].astype(F32)
    for part in parts[1:]:
        total = total + part[...].astype(F32)
    for j in range(2):
        sums[2 * j * count : 2 * (j + 1) * count, :] = total[:, j * width : (j + 1) * width]
    for d, out in enumerate(outs):
        at = pl.ds(pl.multiple_of(((table[0] + d) & 3) * count, count), count)
        out[...] = sums[at, :].astype(out.dtype)


def join(table, own, other, out):
    width = (out.shape[1] - 32) // 2
    for core, (first, second) in enumerate(((own, other), (other, own))):

        @pl.when(table[0] == core)
        def _(first=first, second=second):
            out[:, :width] = first[:, :width]
            out[:, width : 2 * width] = second[:, :width]

    out[:, 2 * width :] = own[:, width:]


def place(table, *refs):
    blocks, outs, choices, rows, routes = refs[:2], refs[2:6], refs[6], refs[7], refs[8]
    count = blocks[0].shape[0]
    width = rows.shape[1]
    picks = (blocks[0].shape[1] - width) // 4
    for k, block in enumerate(blocks):
        at = pl.ds(pl.multiple_of(table[k] * count, count), count)
        rows[at, :] = block[:, :width]
        routes[at, :] = block[:, width:].astype(F32)

    total = rows.shape[0]
    index = lax.broadcasted_iota(jnp.int32, (total, total), 0)
    other = lax.broadcasted_iota(jnp.int32, (total, total), 1)
    earlier = (other < index) & (other // count == index // count)
    earlier = jnp.where(earlier, 1.0, 0.0).astype(BF16)
    ids = routes[:, :picks]
    gates = routes[:, picks : 2 * picks] + (
        routes[:, 2 * picks : 3 * picks] + routes[:, 3 * picks :]
    )
    half = lax.broadcasted_iota(jnp.int32, (total, 1), 0) // count
    places = lax.broadcasted_iota(jnp.int32, (total, 2 * CAPACITY), 1).astype(F32)
    lanes = lax.broadcasted_iota(jnp.int32, (total, 128), 1)
    matches = [ids == table[2 + d].astype(F32) for d in range(4)]
    hits = [
        jnp.max(jnp.where(match, 1.0, 0.0), axis=1, keepdims=True) for match in matches
    ]
    spread = jnp.zeros((total, 128), F32)
    for d, hit in enumerate(hits):
        spread = jnp.where(lanes == d, hit, spread)
    before = dot(earlier, spread.astype(BF16))
    for d, out in enumerate(outs):
        weight = jnp.sum(jnp.where(matches[d], gates, 0.0), axis=1, keepdims=True)
        slot = before[:, d : d + 1] + (half * CAPACITY).astype(F32)
        slot = jnp.where(hits[d] > 0.0, slot, -1.0)
        choices[:, d : d + 1] = slot
        choices[:, 4 + d : 5 + d] = weight
        placing = jnp.where(places == slot, 1.0, 0.0).astype(BF16)
        out[...] = dot(placing, rows[...], ((0,), (0,))).astype(BF16)


def expand(before, table, *refs):
    sums, refs = (refs[0], refs[1:]) if before else (None, refs)
    weights, blocks, out = refs[:4], refs[4:-1], refs[-1]
    hidden = weights[0].shape[2]
    total = sums[...] if before else None
    for i, block in enumerate(blocks):
        weight = jnp.concatenate([weight[table[i]] for weight in weights], axis=1)
        term = dot(block[...], weight)
        total = term if total is None else total + term
    if not before:
        out[...] = total
        return
    for j in range(2):
        gated = total[:, 2 * j * hidden : (2 * j + 1) * hidden]
        upward = total[:, (2 * j + 1) * hidden : (2 * j + 2) * hidden]
        value = gated / (1.0 + jnp.exp(-gated)) * upward
        out[:, j * hidden : (j + 1) * hidden] = value.astype(BF16)


def regroup(table, weight, *outs):
    width = outs[0].shape[2]
    for j in range(8):
        for d, out in enumerate(outs):

            @pl.when(table[j] >> 1 == d)
            def _(j=j, out=out):
                out[table[j] & 1] = weight[:, j * width : (j + 1) * width]


def gather_down(*refs):
    blocks, near, far = refs[:4], refs[4], refs[5]
    for d, block in enumerate(blocks):
        near[d] = block[0]
        far[d] = block[1]


def finish_input(residual, total, *refs):
    parts, routes, out, sent = refs[:3], refs[3], refs[4], refs[5]
    value = residual[...].astype(F32) + total[...]
    for part in parts:
        value = value + part[...].astype(F32)
    width = out.shape[1]
    out[...] = value.astype(BF16)
    sent[:, :width] = value.astype(BF16)
    sent[:, width:] = routes[...]


def contract(near, far, other_near, other_far, *refs):
    blocks, outs = refs[:8], refs[8:]
    total = None
    for i, block in enumerate(blocks):
        own, other = (far, other_far) if i & 1 else (near, other_near)
        term = dot(block[...], jnp.concatenate([own[i >> 1], other[i >> 1]], axis=0))
        total = term if total is None else total + term
    part = outs[0].shape[0]
    for d, out in enumerate(outs):
        out[...] = total[d * part : (d + 1) * part].astype(BF16)


def combine(table, choices, *refs):
    parts, outs, sums = refs[:4], refs[4:8], refs[8]
    total = None
    places = lax.broadcasted_iota(jnp.int32, (choices.shape[0], 2 * CAPACITY), 1).astype(F32)
    for d, block in enumerate(parts):
        weight = jnp.where(places == choices[:, d : d + 1], choices[:, 4 + d : 5 + d], 0.0)
        high = weight.astype(BF16)
        low = (weight - high.astype(F32)).astype(BF16)
        term = dot(high, block[...]) + dot(low, block[...])
        total = term if total is None else total + term
    sums[...] = total
    count, width = outs[0].shape
    for k, out in enumerate(outs):
        at = pl.ds(pl.multiple_of(table[k] * count, count), count)

        @pl.when(table[4 + k] == 0)
        def _(at=at, out=out):
            out[...] = sums[at, :width].astype(BF16)

        @pl.when(table[4 + k] == 1)
        def _(at=at, out=out):
            out[...] = sums[at, width:].astype(BF16)


def struct(*shape, dtype=BF16):
    return jax.ShapeDtypeStruct(shape, dtype)


def tie(value, *others):
    return lax.optimization_barrier((value, *others))[0]


def local(
    queries,
    latents,
    value_up,
    out_proj,
    residual,
    expert_gate,
    expert_up,
    expert_down,
    route_ids,
    route_gates,
):
    tokens, heads, feature_width = queries.shape
    keys = latents.shape[0]
    value_width = value_up.shape[2]
    scale = (value_width + feature_width - value_up.shape[1]) ** (-0.5)
    width = out_proj.shape[1]
    x, z, core = (lax.axis_index(axis) for axis in CTX)
    plane, row = (lax.axis_index(axis) for axis in EP)
    chips = [(((x - dx) & 3), (z ^ dz)) for dx, dz in PLANE]
    owners = [cx * 4 + cz * 2 + (core ^ dk) for dk in range(2) for cx, cz in chips]
    me = x * 4 + z * 2 + core

    first = keys * 16 - tokens * 16 + me * tokens
    b_k = [(plane & 1) ^ k0 for _, k0 in STEPS] + [(plane >> 1) ^ k1 for k1, _ in STEPS]
    entries = {
        "regroup": [(((j >> 1) - x) & 3) * 2 + (z ^ (j & 1)) for j in range(8)],
        "attend": owners + [first],
        "project": [cz * 4 + cx for cx, cz in chips]
        + [((row & 1) ^ k0 ^ core) * 2 + ((row >> 1) ^ k1) for k1, k0 in STEPS],
        "add_parts": [plane],
        "join": [core],
        "combine": b_k,
        "place": [(plane & 1) ^ k0 for k0 in (0, 1)] + [plane * 4 + ((row + d) & 3) for d in range(4)],
        "early": [chips[i][0] * 2 + chips[i][1] for i in EARLY],
        "late": [chips[i][0] * 2 + chips[i][1] for i in LATE],
    }
    starts, table = {}, []
    for name, values in entries.items():
        starts[name] = len(table)
        table += values
    table = jnp.stack(table).astype(jnp.int32)

    rows = jnp.transpose(queries, (1, 0, 2)).reshape(heads * tokens, feature_width)
    gathered = gather_wide(jnp.transpose(latents), [])
    hidden_width = expert_gate.shape[2]
    down = call(
        regroup,
        [struct(2, hidden_width, 2 * width)] * 4,
        start=starts["regroup"],
        name="regroup",
    )(table, expert_down[0])
    down = list(down)
    gathered[6], rows, down[0] = lax.optimization_barrier((gathered[6], rows, down[0]))
    swapped = [shift(block, "core", 1) for block in gathered]
    out_weight = jnp.transpose(out_proj)
    out_swapped = shift(tie(out_weight, *gathered), "core", 1)
    gates = []
    rest = route_gates
    for _ in range(3):
        gates.append(rest.astype(BF16))
        rest = rest - gates[-1].astype(F32)
    routes = jnp.concatenate([route_ids.astype(BF16), *gates], axis=1)

    gate = expert_gate.reshape(8, 2 * width, hidden_width)
    gate_swapped = shift(tie(gate, *swapped), "core", 1)
    down[1] = shift(tie(down[1], *gathered), "x", 1)
    down[3] = shift(tie(down[3], *gathered), "x", 3)
    head_out = call(
        functools.partial(attend, scale, tokens),
        struct(tokens, heads * value_width),
        [pltpu.VMEM((heads * tokens, 16 * keys), F32)],
        vmem=20 << 20,
        flops=10 << 30,
        start=starts["attend"],
        name="attend",
    )(table, rows, value_up, *gathered, *swapped)

    head_out, out_swapped, down[1], down[3], gate_swapped = lax.optimization_barrier(
        (head_out, out_swapped, down[1], down[3], gate_swapped)
    )

    count = route_ids.shape[0]

    gathered_heads = gather_plane(head_out)
    parts = call(
        project,
        [struct(2 * tokens, 2 * width)] * 4,
        [
            pltpu.VMEM((8 * tokens, heads * value_width), BF16),
            pltpu.VMEM((16 * tokens, width), BF16),
        ],
        vmem=16 << 20,
        flops=2 << 30,
        start=starts["project"],
        name="project",
    )(
        table,
        out_weight,
        out_swapped,
        *gathered_heads,
    )
    down[2] = shift(tie(down[2], parts[0]), "x", 2)
    parts = [
        permute(part, ("core", "y"), lambda c, y: (y & 1, ((y >> 1) ^ k1) * 2 + (c ^ k0)))
        for part, (k1, k0) in zip(parts, STEPS)
    ]
    sums = call(
        add_parts,
        [struct(count, width, dtype=F32)] + [struct(count, width)] * 3,
        [pltpu.VMEM((4 * count, width), F32)],
        start=starts["add_parts"],
        name="add_parts",
    )(table, *parts)
    down[2], *sums = lax.optimization_barrier((down[2], *sums))
    near, far = call(
        gather_down, [struct(4, hidden_width, 2 * width)] * 2, name="gather_down"
    )(*down)
    moe_input, routed_input = call(
        finish_input,
        [struct(count, width), struct(count, width + routes.shape[1])],
        name="finish_input",
    )(residual, sums[0], *[shift(sums[d], "z_hi", d) for d in (1, 2, 3)], routes)
    routed_input, near, far = lax.optimization_barrier((routed_input, near, far))

    joined = call(
        join, struct(count, 2 * width + routes.shape[1]), start=starts["join"], name="join"
    )(table, routed_input, shift(routed_input, "core", 1))
    planes = [
        permute(joined, ("core", "z_hi"), lambda c, p: (p >> 1, 2 * c + (k0 ^ (p & 1))))
        for k0 in (0, 1)
    ]
    *outgoing, choices = call(
        place,
        [struct(2 * CAPACITY, 2 * width)] * 4 + [struct(2 * count, 8, dtype=F32)],
        [pltpu.VMEM((2 * count, 2 * width), BF16), pltpu.VMEM((2 * count, routes.shape[1]), F32)],
        start=starts["place"],
        name="place",
    )(table, *planes)
    arrived = [outgoing[0]] + [shift(outgoing[d], "y", d) for d in (1, 2, 3)]
    arrived = jnp.concatenate(arrived, axis=0)
    up, near = lax.optimization_barrier((expert_up, near, arrived))[:2]
    up = up.reshape(8, 2 * width, hidden_width)
    swapped = [shift(up, "core", 1)]
    slots = gather_wide(arrived, swapped)
    (up_swapped,) = swapped
    far = shift(tie(far, slots[1]), "z_lo", 1)
    near_swapped = shift(tie(near, slots[1]), "core", 1)

    weights = (gate, up, gate_swapped, up_swapped)
    part = struct(8 * CAPACITY, 4 * hidden_width, dtype=F32)
    hidden = ()
    last = struct(8 * CAPACITY, 2 * hidden_width)
    for name, some, out in (("early", EARLY, part), ("late", LATE, last)):
        hidden = call(
            functools.partial(expand, len(hidden)),
            out,
            vmem=16 << 20,
            flops=len(some) * (512 << 20),
            start=starts[name],
            name="expand",
        )(table, *hidden, *weights, *[slots[i] for i in some])
        hidden = (hidden,)
    (hidden,) = hidden
    hidden, near_swapped, far = lax.optimization_barrier((hidden, near_swapped, far))
    far_swapped = shift(far, "core", 1)
    hidden = gather_plane(hidden)
    results = call(
        contract,
        [struct(2 * CAPACITY, 2 * width)] * 4,
        vmem=16 << 20,
        flops=2 << 30,
        name="contract",
    )(near, far, near_swapped, far_swapped, *hidden)

    returned = [results[0]] + [shift(results[d], "y", -d) for d in (1, 2, 3)]
    sums = call(
        combine,
        [struct(count, width)] * 4,
        [pltpu.VMEM((2 * count, 2 * width), F32)],
        start=starts["combine"],
        name="combine",
    )(table, choices, *returned)
    routed = None
    for part, (k1, k0) in zip(sums, STEPS):
        part = permute(
            part,
            ("core", "z_hi"),
            lambda c, p: (p >> 1, ((c ^ k1) << 1) | ((p & 1) ^ k0)),
        ).astype(F32)
        routed = part if routed is None else routed + part
    return (moe_input.astype(F32) + routed).astype(BF16)


def solution(mesh):
    split = Mesh(mesh.devices.reshape(tuple(SIZES.values())), tuple(SIZES))
    return jax.shard_map(
        local,
        mesh=split,
        in_specs=(
            P(CTX, EP, None),
            P(CTX, None),
            P(EP, None, None),
            P(EP, CTX),
            P(EP, CTX),
            P(EP, None, CTX),
            P(EP, None, CTX),
            P(EP, CTX, None),
            P(EP, None),
            P(EP, None),
        ),
        out_specs=P(EP, CTX),
        check_vma=False,
    )
```
